32 devices in a mesh: cols: 8 (over z, y), mem: 4 (over x, core).
Axes of the slice: x: 2, y: 2, z: 4, core: 2. Of those that a mesh axis runs over, the one named last changes fastest.
Arguments:
- state: float32 [80, 262144], P('mem', 'cols'), may hold values from -6 to 6
- obs_value: float32 [4, 1024], P(None, 'cols'), may hold values from -6 to 6
- obs_var: float32 [4, 1024], P(None, 'cols'), may hold values from 0.2 to 2
- owner: int32 [4, 1024, 1], P(None, 'cols'), may hold values from 0 to 7; in each aligned block of 128 rows (0 to 127, 128 to 255, ..., all dimensions but the last counted through in order) at most 32 rows name the same one
- tile_of: int32 [4, 1024], P(None, 'cols'), may hold values from 0 to 63
- offsets: int32 [4, 1024, 4], P(None, 'cols'), may hold values from 0 to 511
- accept: int32 [4, 1024], P(None, 'cols'), may hold values 0 or 1
- loc_mask: int32 [512, 4, 8], P(('cols', 'mem')), may hold values 0 or 1
Outputs:
- posterior: float32 [80, 262144], P(None, ('cols', 'mem'))
The draws below stay inside these ranges and needn't reach their ends.
Inputs may be any that keep to these rules, and one draw needn't show every extreme that they name: Within the 128 observations of one batch held by one index of cols, no owner is named more than 32 times, and that many is reached.
All inputs are finite; a program needn't handle non-finite values. No bound on the sum of `accept` or of `loc_mask` on one device may be relied on, other than what follows from the above.
Results may differ from the reference program's by a relative error of at most 0.0002.
Values sent between devices are 32-bit elements; how exact they have to be, the bound alone decides.
No kernel may reach another device: no remote copies, remote signals or barrier semaphores. Data moves between devices by JAX's collectives and lax.ppermute only.
A program may use at most 64 MiB of HBM per device.

```python
import math
import jax
import jax.numpy as jnp
import numpy as np
from jax import lax

M = 80
NS_DEV = 32768
NB = 4
KB = 1024
P_SIZE = 4
TILE = 512
OBLK = 128
NS = 262144
KS = 128
SCAP = 32
TPS = 64
NTILES = 512
NBLK = 8
N_COLS = 8


def set_ends(entries, rng, low, top_value):
    longest = entries.shape.index(max(entries.shape))
    spots = []
    for shift in (0, 1):
        where = [jax.random.randint(jax.random.fold_in(rng, axis), (), 0, length) for axis, length in enumerate(entries.shape)]
        where[longest] = (where[longest] + shift) % entries.shape[longest]
        spots.append(tuple(where))
    return entries.at[spots[0]].set(low).at[spots[1]].set(top_value)


def level_of(stream_key, dims, cuts, smallest, high):
    def one(dim, parts):
        steps = jax.random.uniform(jax.random.fold_in(jax.random.fold_in(stream_key, 6), dim), (parts,), jnp.float32, smallest / len(cuts), high / len(cuts))
        return jnp.repeat(jnp.exp(steps), dims[dim] // parts).reshape((-1,) + (1,) * (len(dims) - dim - 1))

    loudness = one(*cuts[0])
    for cut in cuts[1:]:
        loudness = loudness * one(*cut)
    return loudness


def shared_out(stream_key, own, number, rows, amount, top, bound, slope):
    sequence = jax.random.permutation(stream_key, amount)
    crowded, common = portions_of(amount, rows * top, bound, slope, True), portions_of(amount, rows * top, bound, slope, False)
    places = jnp.arange(amount)

    def named(lengths, offset_by):
        used = int((lengths > 0).sum())
        fixed = max(1, used // 4)
        moved = fixed + (places - fixed + offset_by * (used - fixed)) % max(1, amount - fixed)
        return jnp.zeros((amount,), jnp.int32).at[sequence[jnp.where(places < fixed, places, moved)]].set(jnp.asarray(lengths, jnp.int32))

    lengths = jnp.where(number % 4 == 0, named(crowded, number // 4), named(common, number - number // 4 - 1))
    mixed = jax.random.permutation(jax.random.fold_in(own, 3), amount)
    donor, sink = mixed[0:amount // 2 * 2:2], mixed[1:amount // 2 * 2:2]
    room = jnp.minimum(lengths[donor] - 1, bound - lengths[sink]) // 2
    room = jnp.where((donor == sequence[0]) | (sink == sequence[0]) | (lengths[sink] == 0), 0, jnp.maximum(room, 0))
    moved = jax.random.randint(jax.random.fold_in(own, 4), (amount // 2,), 0, 1 << 20) % (room + 1)
    lengths = lengths.at[donor].add(-moved).at[sink].add(moved)
    items = jnp.searchsorted(jnp.cumsum(lengths), jnp.arange(rows * top), side="right").astype(jnp.int32)
    listing = items.reshape(top, rows).T
    listing = listing[jax.random.permutation(jax.random.fold_in(own, 1), rows)]
    offset_by = jax.random.randint(jax.random.fold_in(own, 2), (rows, 1), 0, top)
    return jnp.take_along_axis(listing, (jnp.arange(top)[None, :] + offset_by) % top, axis=1)


def portions_of(count, total, limit, lean, full):
    portions = [(1 << 20) // math.isqrt(standing ** lean) + 1 for standing in range(1, count + 1)]
    largest = limit if full else min(limit, max(-(-total // count), total * portions[0] // sum(portions)))
    least = 1 if total - largest >= count - 1 else 0
    given, rest = [largest] + [least] * (count - 1), total - largest - least * (count - 1)
    while rest > 0:
        candidates = [i for i in range(1, count) if given[i] < largest] or [i for i in range(1, count) if given[i] < limit]
        mass, budget = sum([portions[i] for i in candidates]), rest
        for i in candidates:
            more = min(limit - given[i], max(1, budget * portions[i] // mass), rest)
            given[i] = given[i] + more
            rest = rest - more
    return np.array(given)


def scatter_about(own_key, shape, width, limit, shards=(), kind=jnp.bfloat16):
    result = jax.random.normal(own_key, shape, jnp.float32) * width
    if len(shards) > 0:
        result = level_of(own_key, shape, shards, -0.22, 0.18) * result
    return jnp.clip(result, min=-limit, max=limit).astype(kind)


def setup_inputs(seed: int = 0) -> dict:
    arg_keys = jax.random.split(jax.random.key(seed), 9)
    state = scatter_about(arg_keys[0], (M, NS), 1.0, 6.0, ((0, 4), (1, 8)), jnp.float32)
    obs_value = scatter_about(arg_keys[1], (NB, KB), 1.0, 6.0, ((1, 8),), jnp.float32)
    obs_var = jnp.clip(jnp.exp(math.log(2.0) - 2.3025851 * jax.random.uniform(arg_keys[2], (NB, KB), jnp.float32) ** level_of(arg_keys[2], (NB, KB), ((1, 8),), -0.2, 0.2)), 0.2, 2.0)
    owner_keys = jax.random.split(jax.random.fold_in(arg_keys[3], 1), NB * KB // KS)
    owner_turns = jax.random.permutation(jax.random.fold_in(arg_keys[3], 3), NB * KB // KS)
    owner = jax.vmap(lambda own, number: shared_out(jax.random.fold_in(arg_keys[3], 2), own, number, KS, N_COLS, 1, SCAP, 2))(owner_keys, owner_turns).reshape((NB, KB, 1))
    tile_of = set_ends(jax.random.randint(arg_keys[4], (NB, KB), 0, TPS), jax.random.fold_in(arg_keys[4], 1), 0, TPS - 1).astype(jnp.int32)
    offsets = set_ends(jax.random.randint(arg_keys[5], (NB, KB, P_SIZE), 0, TILE), jax.random.fold_in(arg_keys[5], 1), 0, TILE - 1).astype(jnp.int32)
    accept = set_ends((jax.random.randint(arg_keys[6], (NB, KB), 0, 10) < 9).astype(jnp.int32), jax.random.fold_in(arg_keys[6], 1), 0, 1)
    loc_mask = set_ends((jax.random.randint(arg_keys[7], (NTILES, NB, NBLK), 0, 4) < 1).astype(jnp.int32), jax.random.fold_in(arg_keys[7], 1), 0, 1)
    return {"state": state, "obs_value": obs_value, "obs_var": obs_var, "owner": owner, "tile_of": tile_of, "offsets": offsets, "accept": accept, "loc_mask": loc_mask}


epsilon = 1e-05
EXACT = lax.Precision.HIGHEST

def innovations(prior_obs, observed, obs_noise, accepted):
    members = prior_obs.shape[0]
    mean_prior = lax.optimization_barrier(jnp.mean(prior_obs, axis=0))
    spread = prior_obs - mean_prior
    spread_var = lax.optimization_barrier(jnp.sum(spread * spread, axis=0)) / (members - 1) + epsilon
    denominator = spread_var + obs_noise
    mean_shift = spread_var / denominator * (observed - mean_prior)
    factor = jnp.sqrt(obs_noise / denominator) - 1.0
    increment = accepted * (mean_shift + factor * spread)
    scaled = spread / ((members - 1) * spread_var)
    return (increment, scaled)

def reference(state, obs_value, obs_var, owner, tile_of, offsets, accept, loc_mask):
    ensemble = state
    for batch_no in range(NB):
        cells_of = (owner[batch_no, :, 0] * NS_DEV + tile_of[batch_no] * TILE).astype(jnp.int32)[:, None] + offsets[batch_no]
        picked = jnp.take(ensemble, cells_of.reshape(-1).astype(jnp.int32), axis=1).reshape(M, KB, P_SIZE)
        prior_obs = lax.optimization_barrier(jnp.sum(picked, axis=2)) / P_SIZE
        increment, scaled = innovations(prior_obs, obs_value[batch_no], obs_var[batch_no], accept[batch_no].astype(jnp.float32))
        per_block = jnp.einsum('nbk,mbk->bnm', scaled.reshape(M, NBLK, OBLK), increment.reshape(M, NBLK, OBLK), precision=EXACT)
        mixing = jnp.einsum('tb,bnm->tnm', loc_mask[:, batch_no, :].astype(jnp.float32), per_block, precision=EXACT)
        mean_state = lax.optimization_barrier(jnp.mean(ensemble, axis=0))
        deviation = (ensemble - mean_state).reshape(M, NTILES, TILE)
        change = jnp.einsum('tnm,nti->mti', mixing, deviation, precision=EXACT)
        ensemble = ensemble + change.reshape(M, NS)
    return ensemble
```

```python
import functools

import jax
import jax.numpy as jnp
from jax import lax
from jax.experimental import pallas as pl
from jax.experimental.pallas import tpu as pltpu
from jax.sharding import PartitionSpec as P

epsilon = 1e-05
EXACT = lax.Precision.HIGHEST
f32, bf16, i32 = jnp.float32, jnp.bfloat16, jnp.int32
LANES = 128
CHUNK = 256
TILE = 512
PAD = 24
WHOLE = pl.BlockSpec()
FAR = pl.BlockSpec(memory_space=pltpu.HBM)
PARAMS = pltpu.CompilerParams(vmem_limit_bytes=48 * 1024 * 1024)


def iota(shape, axis):
    return lax.broadcasted_iota(i32, shape, axis)


def dot(a, b, dims):
    return lax.dot_general(a, b, ((dims[0], dims[1]), ((), ())), preferred_element_type=f32)


def two(x):
    high = x.astype(bf16)
    return high, (x - high.astype(f32)).astype(bf16)


def slot_rows(sid, slots):
    return jnp.where(iota((slots, sid.shape[1]), 0) == sid, 1.0, 0.0).astype(bf16)


def route_kernel(owners, slots_per, *refs):
    ins, (msg_ref, sid_ref), here, sems = refs[0:7], refs[7:9], refs[9:16], refs[16]
    copies = [pltpu.make_async_copy(a, b, sems.at[i]) for i, (a, b) in enumerate(zip(ins, here))]
    for copy in copies:
        copy.start()
    for copy in copies:
        copy.wait()
    owner_ref, tile_ref, off_ref, val_ref, var_ref, acc_ref, mask_ref = here
    batches, _, per = owner_ref.shape
    slots = owners * slots_per
    hot = [
        jnp.where(iota((owners, per), 0) == owner_ref[b], 1.0, 0.0) for b in range(batches)
    ]
    before = jnp.where(iota((per, per), 0) < iota((per, per), 1), 1.0, 0.0).astype(bf16)
    counts = dot(jnp.concatenate(hot, axis=0).astype(bf16), before, ((1,), (0,)))
    used = jnp.zeros((owners, 1), f32)
    total = jnp.zeros((16, slots), f32)
    for b in range(batches):
        own = owner_ref[b]
        rank = used + counts[b * owners : (b + 1) * owners]
        rank = jnp.sum(hot[b] * rank, axis=0, keepdims=True)
        used = used + jnp.sum(hot[b], axis=1, keepdims=True)
        sid = own * slots_per + rank.astype(i32)
        sid_ref[b : b + 1, :] = sid
        cells = tile_ref[b : b + 1, :] * 512 + off_ref[b]
        fields = jnp.concatenate(
            [(cells >> 7).astype(f32), (cells & 127).astype(f32), jnp.ones((8, per), f32)], axis=0
        ).astype(bf16)
        total = total + dot(fields, slot_rows(sid, slots), ((1,), (1,)))
    cells = total[0:4] * 128.0 + total[4:8] + (total[8:12] - 1.0)
    tiles = mask_ref.shape[1]
    kinds = mask_ref.shape[0]
    spread_out = jnp.where(iota((kinds, LANES), 0) == (iota((kinds, LANES), 1) & (kinds - 1)), 1.0, 0.0)
    wide = dot(mask_ref[...].astype(bf16), spread_out.astype(bf16), ((0,), (0,)))
    group = LANES // kinds
    lane_tile = iota((tiles, LANES), 1) // kinds
    masks = [
        jnp.sum(jnp.where(iota((tiles, LANES), 0) == lane_tile + r * group, wide, 0.0), axis=0, keepdims=True)
        for r in range(tiles // group)
    ]
    owner = jnp.concatenate([owner_ref[b] for b in range(batches)], axis=0)
    where_tile = (owner * 64 + tile_ref[...]).astype(f32)
    shared = jnp.concatenate(
        [val_ref[...], var_ref[...], acc_ref[...].astype(f32), where_tile] + masks, axis=0
    )
    for c in range(owners):
        msg_ref[c, 0:4, :] = cells[:, c * slots_per : (c + 1) * slots_per]
        msg_ref[c, 4:24, :] = shared


def prepare_kernel(state_ref, out_ref):
    rows = state_ref.shape[0]
    fill = jnp.zeros((PAD - rows, TILE), f32)
    for t in range(state_ref.shape[1] // TILE):
        tile = jnp.concatenate([state_ref[:, t * TILE : (t + 1) * TILE], fill], axis=0)
        high = tile.astype(bf16).astype(f32)
        out_ref[t * 2 * PAD : (t + 1) * 2 * PAD, :] = jnp.concatenate([high, tile - high], axis=0).astype(bf16)


def pick_kernel(rows, msg_ref, parts_ref, out_ref, mask_ref, weight_ref):
    homes, _, slots_per = msg_ref.shape
    tiles = parts_ref.shape[0] // (2 * PAD)
    each = CHUNK // slots_per
    mask_ref[...] = msg_ref[:, 20:24, :]
    for g in range(homes // each):
        cells = jnp.concatenate([msg_ref[g * each + i, 0:4, :] for i in range(each)], axis=1)
        cells = jnp.maximum(cells.astype(i32), 0)
        weight = jnp.zeros((TILE, CHUNK), f32)
        for p in range(4):
            weight = weight + jnp.where(iota((TILE, CHUNK), 0) == (cells[p : p + 1] & (TILE - 1)), 0.25, 0.0)
        weight_ref[...] = weight.astype(bf16)
        tile = cells[0:1] >> 9
        sums = dot(parts_ref[...], weight_ref[...], ((1,), (0,)))
        total = jnp.zeros((PAD, CHUNK), f32)
        for t in range(tiles):
            both = sums[t * 2 * PAD : t * 2 * PAD + PAD] + sums[t * 2 * PAD + PAD : (t + 1) * 2 * PAD]
            total = total + jnp.where(tile == t, both, 0.0)
        for i in range(each):
            out_ref[g * each + i] = total[0:rows, i * slots_per : (i + 1) * slots_per]


def place_kernel(got_ref, sid_ref, keep_ref, send_ref):
    owners, rows, slots_per = got_ref.shape
    batches, per = sid_ref.shape
    slots = owners * slots_per
    core = lax.axis_index("mem") & 1
    fill = jnp.zeros((24 - rows, slots), f32)
    got = jnp.concatenate([got_ref[c] for c in range(owners)], axis=1)
    got = jnp.concatenate([got, fill], axis=0)
    first = got.astype(bf16).astype(f32)
    rest = got - first
    second = rest.astype(bf16).astype(f32)
    parts = jnp.concatenate([first, second, rest - second], axis=0).astype(bf16)
    half = batches // 2
    for ref, which in ((keep_ref, core), (send_ref, 1 - core)):
        for i in range(half):
            sid = jnp.where(which == 0, sid_ref[i : i + 1, :], sid_ref[half + i : half + i + 1, :])
            out = dot(parts, slot_rows(sid, slots), ((1,), (0,)))
            out = out[0:24] + out[24:48] + out[48:72]
            ref[:, i * per : (i + 1) * per] = out[0:rows]


def mask_kernel(tiles, members, info_ref, a_ref, b_ref, c_ref, d_ref, mask_ref):
    homes = info_ref.shape[0]
    mem = lax.axis_index("mem")
    device = lax.axis_index("cols") * lax.axis_size("mem") + mem
    table = [ref[h] for ref in (a_ref, b_ref, c_ref, d_ref) for h in range(homes)]
    table = jnp.concatenate(table, axis=0).astype(bf16)
    kinds = mask_ref.shape[1]
    group = LANES // kinds
    obs_chunks = 16
    for idx in range(mask_ref.shape[0]):
        if idx < obs_chunks:
            b, h = idx // 4, 2 * (idx % 4)
            where_tile = jnp.concatenate([info_ref[h, 16 + b : 17 + b, :], info_ref[h + 1, 16 + b : 17 + b, :]], axis=1)
            where_tile = where_tile.astype(i32)
        else:
            column = iota((1, CHUNK), 1) + (idx - obs_chunks) * CHUNK
            where_tile = jnp.zeros((1, CHUNK), i32) + device * tiles
            for t in range(1, tiles):
                where_tile = where_tile + jnp.where(column >= t * members, 1, 0)
        row = ((((where_tile >> 4) & 3) ^ mem) * homes + (where_tile >> 6)) * 4 + ((where_tile >> 2) & 3)
        hot = jnp.where(iota((LANES, CHUNK), 0) == row, 1.0, 0.0).astype(bf16)
        rows = dot(table, hot, ((0,), (0,)))
        out = jnp.zeros((kinds, CHUNK), f32)
        for g in range(group):
            out = out + jnp.where((where_tile & 3) == g, rows[g * kinds : (g + 1) * kinds], 0.0)
        mask_ref[idx] = out


def split_kernel(*refs):
    own, near, pieces, out_ref = refs[0], refs[1], refs[2:-1], refs[-1]
    rows = own.shape[0]
    begin = 0
    for i in range(0, len(pieces), 2):
        end = begin + pieces[i].shape[1]
        cells = slice(begin, end)
        whole = jnp.concatenate([own[:, cells], near[:, cells], pieces[i][...], pieces[i + 1][...]], axis=0)
        high, low = two(whole)
        out_ref[0 : 4 * rows, cells] = high
        out_ref[4 * rows : 8 * rows, cells] = low
        begin = end


def window_kernel(tiles, rows, mm_ref, mx_ref, cm_ref, cx_ref, info_ref, mask_ref, ens_ref, out_ref, y_ref, w_ref):
    homes, half_members, wide = mm_ref.shape
    members = 2 * half_members
    per = wide // 2
    batches = 4
    blocks = homes
    mem = lax.axis_index("mem")
    x, core = mem >> 1, mem & 1
    obs_chunks = batches * homes * per // CHUNK
    x_chunks = tiles * members // CHUNK
    for b in range(batches):
        lanes = slice((b % 2) * per, (b % 2 + 1) * per)
        mine = core == b // 2
        for h in range(homes):
            near = jnp.where(mine, mm_ref[h, :, lanes], cm_ref[h, :, lanes])
            far = jnp.where(mine, mx_ref[h, :, lanes], cx_ref[h, :, lanes])
            chunk, place = b * (homes // 2) + h // 2, (h % 2) * per
            y_ref[chunk, 0:half_members, place : place + per] = jnp.where(x == 0, near, far)
            y_ref[chunk, half_members:members, place : place + per] = jnp.where(x == 0, far, near)
    member = iota((members, CHUNK), 0)
    for q in range(x_chunks):
        column = iota((1, CHUNK), 1) + q * CHUNK
        tile = jnp.zeros((1, CHUNK), i32)
        for t in range(1, tiles):
            tile = tile + jnp.where(column >= t * members, 1, 0)
        column = column - tile * members
        part = jnp.zeros((1, CHUNK), i32)
        for k in range(1, 4):
            part = part + jnp.where(column >= k * rows, 1, 0)
        true = column - part * rows + (part ^ mem) * rows
        y_ref[obs_chunks + q] = jnp.where(member == true, 1.0, 0.0)

    lane3 = iota((members, 3 * members), 1)
    for b in range(batches):
        for g in range(homes // 2):
            def field(f):
                return jnp.concatenate(
                    [info_ref[h, 4 + 4 * f + b : 5 + 4 * f + b, :] for h in (2 * g, 2 * g + 1)], axis=1
                )

            prior = y_ref[b * (homes // 2) + g]
            mean = jnp.sum(prior, axis=0, keepdims=True) / members
            spread = prior - mean
            var = jnp.sum(spread * spread, axis=0, keepdims=True) / (members - 1) + epsilon
            noise = field(1)
            denominator = var + noise
            shift = var / denominator * (field(0) - mean)
            factor = jnp.sqrt(noise / denominator) - 1.0
            increment = field(2) * (shift + factor * spread)
            scaled = spread / ((members - 1) * var)
            ih, il = two(increment)
            sh, sl = two(scaled)
            for i in range(2):
                lanes = slice(i * per, (i + 1) * per)
                left = jnp.concatenate([ih[:, lanes], ih[:, lanes], il[:, lanes]], axis=1)
                right = jnp.concatenate([sh[:, lanes], sl[:, lanes], sh[:, lanes]], axis=1)
                right = jnp.concatenate([right, right, right], axis=0)
                block = dot(left, right, ((1,), (1,)))
                high = block.astype(bf16).astype(f32)
                block = jnp.where(lane3 < 2 * members, high, block - high)
                h = 2 * g + i
                w_ref[h * members : (h + 1) * members, :] = block.astype(bf16)

        def update(idx, carry, b=b):
            now = y_ref[idx]
            deviation = now - jnp.sum(now, axis=0, keepdims=True) / members
            dh, dl = two(deviation)
            moved = dot(w_ref[...], jnp.concatenate([dh, dl, dh], axis=0), ((1,), (0,)))
            for k in range(blocks):
                now = now + mask_ref[idx, b * blocks + k : b * blocks + k + 1, :] * moved[
                    k * members : (k + 1) * members
                ]
            y_ref[idx] = now
            return carry

        lax.fori_loop((b + 1) * (homes // 2), obs_chunks + x_chunks, update, 0)

    size = out_ref.shape[1] // tiles
    flat = jnp.concatenate([y_ref[obs_chunks + q] for q in range(x_chunks)], axis=1)
    for t in range(tiles):
        weight = flat[:, t * members : (t + 1) * members]
        high = weight.astype(bf16).astype(f32)
        weight = jnp.concatenate([high, high, weight - high], axis=1).astype(bf16)
        cells = slice(t * size, (t + 1) * size)
        ens_high, ens_low = ens_ref[0:members, cells], ens_ref[members : 2 * members, cells]
        out_ref[:, cells] = dot(weight, jnp.concatenate([ens_high, ens_low, ens_high], axis=0), ((1,), (0,)))


def fast(state, obs_value, obs_var, owner, tile_of, offsets, accept, loc_mask):
    owners = lax.axis_size("cols")
    mem_devices = lax.axis_size("mem")
    mem = lax.axis_index("mem")
    core = mem & 1
    batches, per = obs_value.shape
    rows, slab = state.shape
    members = rows * mem_devices
    cells = slab // mem_devices
    tiles = loc_mask.shape[0]
    kinds = loc_mask.shape[1] * loc_mask.shape[2]
    cap = 2 * per // owners
    slots_per = batches * cap

    about = (
        owner.transpose(0, 2, 1),
        tile_of,
        offsets.transpose(0, 2, 1),
        obs_value,
        obs_var,
        accept,
        loc_mask.transpose(1, 2, 0).reshape(kinds, tiles),
    )
    msg, sid = pl.pallas_call(
        functools.partial(route_kernel, owners, slots_per),
        out_shape=(
            jax.ShapeDtypeStruct((owners, 24, slots_per), f32),
            jax.ShapeDtypeStruct((batches, per), i32),
        ),
        in_specs=[FAR] * 7,
        out_specs=(WHOLE,) * 2,
        scratch_shapes=[pltpu.VMEM(a.shape, a.dtype) for a in about] + [pltpu.SemaphoreType.DMA((7,))],
        compiler_params=PARAMS,
        name="route",
    )(*about)
    arrived = lax.all_to_all(msg, "cols", split_axis=0, concat_axis=0, tiled=True)

    parts = pl.pallas_call(
        prepare_kernel,
        out_shape=jax.ShapeDtypeStruct((slab // TILE * 2 * PAD, TILE), bf16),
        in_specs=[WHOLE],
        out_specs=WHOLE,
        compiler_params=PARAMS,
        name="prepare",
    )(state)
    own = lax.dynamic_slice_in_dim(state, mem * cells, cells, 1)

    def swap(array, k):
        return lax.ppermute(array, "mem", [(i, i ^ k) for i in range(4)])

    def piece(begin, width):
        return [swap(lax.dynamic_slice_in_dim(state, (mem ^ k) * cells + begin, width, 1), k) for k in (2, 3)]

    near = swap(lax.dynamic_slice_in_dim(state, (mem ^ 1) * cells, cells, 1), 1)
    first = piece(0, 2048)
    second = piece(2048, 2048)
    third = piece(4096, 4096)
    arrived, near, *first = lax.optimization_barrier((arrived, near, *first))
    priors, mask = pl.pallas_call(
        functools.partial(pick_kernel, rows),
        out_shape=(
            jax.ShapeDtypeStruct((owners, rows, slots_per), f32),
            jax.ShapeDtypeStruct((owners, 4, LANES), f32),
        ),
        in_specs=[WHOLE] * 2,
        out_specs=(WHOLE,) * 2,
        scratch_shapes=[pltpu.VMEM((TILE, CHUNK), bf16)],
        compiler_params=PARAMS,
        name="pick",
    )(arrived, parts)
    tables = [mask] + [swap(mask, k) for k in (1, 2, 3)]
    at_home = lax.all_to_all(priors, "cols", split_axis=0, concat_axis=0, tiled=True)
    at_home, *second = lax.optimization_barrier((at_home, *second))
    keep, send = pl.pallas_call(
        place_kernel,
        out_shape=(jax.ShapeDtypeStruct((rows, batches // 2 * per), f32),) * 2,
        in_specs=[WHOLE] * 2,
        out_specs=(WHOLE,) * 2,
        compiler_params=PARAMS,
        name="place",
    )(at_home, sid)
    got = swap(send, 1)
    chip = jnp.where(
        core == 0, jnp.concatenate([keep, got], axis=0), jnp.concatenate([got, keep], axis=0)
    )
    everyone = jnp.broadcast_to(chip[None], (owners,) + chip.shape)
    mine = lax.all_to_all(everyone, "cols", split_axis=0, concat_axis=0, tiled=True)
    mine, *third = lax.optimization_barrier((mine, *third))
    over_x = swap(mine, 2)
    cm, cx = swap(mine, 1), swap(over_x, 1)

    obs_chunks = batches * owners * per // CHUNK
    x_chunks = tiles * members // CHUNK
    masks = pl.pallas_call(
        functools.partial(mask_kernel, tiles, members),
        out_shape=jax.ShapeDtypeStruct((obs_chunks + x_chunks, kinds, CHUNK), f32),
        in_specs=[WHOLE] * 5,
        out_specs=WHOLE,
        compiler_params=PARAMS,
        name="masks",
    )(arrived, *tables)
    pieces = pl.pallas_call(
        split_kernel,
        out_shape=jax.ShapeDtypeStruct((2 * members, cells), bf16),
        in_specs=[WHOLE] * 8,
        out_specs=WHOLE,
        compiler_params=PARAMS,
        name="split",
    )(own, near, *first, *second, *third)
    return pl.pallas_call(
        functools.partial(window_kernel, tiles, rows),
        out_shape=jax.ShapeDtypeStruct((members, cells), f32),
        in_specs=[WHOLE] * 7,
        out_specs=WHOLE,
        scratch_shapes=[
            pltpu.VMEM((obs_chunks + x_chunks, members, CHUNK), f32),
            pltpu.VMEM((owners * members, 3 * members), bf16),
        ],
        compiler_params=PARAMS,
        name="window",
    )(mine, over_x, cm, cx, arrived, masks, pieces)


def innovations(prior_obs, observed, obs_noise, accepted):
    members = prior_obs.shape[0]
    mean_prior = jnp.mean(prior_obs, axis=0)
    spread = prior_obs - mean_prior
    spread_var = jnp.sum(spread * spread, axis=0) / (members - 1) + epsilon
    denominator = spread_var + obs_noise
    mean_shift = spread_var / denominator * (observed - mean_prior)
    factor = jnp.sqrt(obs_noise / denominator) - 1.0
    increment = accepted * (mean_shift + factor * spread)
    scaled = spread / ((members - 1) * spread_var)
    return (increment, scaled)


def plain(state, obs_value, obs_var, owner, tile_of, offsets, accept, loc_mask):
    col_devices = lax.axis_size("cols")
    mem_devices = lax.axis_size("mem")
    source = lax.axis_index("cols")
    mem_index = lax.axis_index("mem")
    batch_total, per_src = obs_value.shape
    pick_count = offsets.shape[2]
    members = state.shape[0] * mem_devices
    cell_count = state.shape[1] // mem_devices
    tiles_here = loc_mask.shape[0]
    tile_len = cell_count // tiles_here
    block_count = loc_mask.shape[2]
    batch_obs = per_src * col_devices
    block_len = batch_obs // block_count
    capacity = max(2, 2 * per_src // col_devices)
    slot_count = col_devices * capacity
    destination = owner[:, :, 0]
    ordinal = jnp.arange(per_src, dtype=jnp.int32)
    same_owner = destination[:, :, None] == destination[:, None, :]
    earlier = (ordinal[None, :] < ordinal[:, None])[None]
    slot_rank = jnp.sum((same_owner & earlier).astype(jnp.int32), axis=2)
    batch_rows = jnp.broadcast_to(
        jnp.arange(batch_total, dtype=jnp.int32)[:, None], destination.shape
    )
    position = jnp.broadcast_to(source * per_src + ordinal, destination.shape)
    fields = jnp.concatenate(
        [tile_of[:, :, None], accept[:, :, None], position[:, :, None], offsets], axis=2
    )
    blank_int = (
        jnp.zeros((batch_total, col_devices, capacity, 3 + pick_count), jnp.int32)
        .at[:, :, :, 2]
        .set(-1)
    )
    sent_int = blank_int.at[batch_rows, destination, slot_rank].set(fields)
    blank_val = (
        jnp.zeros((batch_total, col_devices, capacity, 2), jnp.float32).at[:, :, :, 1].set(1.0)
    )
    sent_val = blank_val.at[batch_rows, destination, slot_rank].set(
        jnp.stack([obs_value, obs_var], axis=2)
    )
    arrived_int = lax.all_to_all(sent_int, "cols", split_axis=1, concat_axis=1, tiled=True).reshape(
        batch_total, slot_count, 3 + pick_count
    )
    arrived_val = lax.all_to_all(sent_val, "cols", split_axis=1, concat_axis=1, tiled=True).reshape(
        batch_total, slot_count, 2
    )
    obs_tile = arrived_int[:, :, 0]
    obs_flag = arrived_int[:, :, 1].astype(jnp.float32)
    obs_pos = arrived_int[:, :, 2]
    obs_off = arrived_int[:, :, 3:]
    observed = arrived_val[:, :, 0]
    obs_noise = arrived_val[:, :, 1]
    targets = jnp.where(obs_pos >= 0, obs_pos, batch_obs)
    ensemble = lax.all_to_all(state, "mem", split_axis=1, concat_axis=0, tiled=True)
    for batch_no in range(batch_total):
        local_cell = (
            obs_tile[batch_no][:, None] * tile_len + obs_off[batch_no] - mem_index * cell_count
        )
        inside = (local_cell >= 0) & (local_cell < cell_count) & (obs_pos[batch_no] >= 0)[:, None]
        flat_cells = jnp.clip(local_cell, 0, cell_count - 1).reshape(-1)
        picked = jnp.take(ensemble, flat_cells, axis=1).reshape(members, slot_count, pick_count)
        prior_obs = lax.psum(
            jnp.sum(jnp.where(inside[None], picked, 0.0), axis=2) / pick_count, "mem"
        )
        increment, scaled = innovations(
            prior_obs, observed[batch_no], obs_noise[batch_no], obs_flag[batch_no]
        )
        blank_panel = jnp.zeros((members, batch_obs), jnp.float32)
        placed_inc = blank_panel.at[:, targets[batch_no]].add(increment, mode="drop")
        placed_scl = blank_panel.at[:, targets[batch_no]].add(scaled, mode="drop")
        inc_all, scl_all = lax.psum((placed_inc, placed_scl), "cols")
        mask_now = loc_mask[:, batch_no, :].astype(jnp.float32)
        mean_state = jnp.mean(ensemble, axis=0)
        deviation = (ensemble - mean_state).reshape(members, tiles_here, tile_len)
        per_block = jnp.einsum(
            "nbk,mbk->bnm",
            scl_all.reshape(members, block_count, block_len),
            inc_all.reshape(members, block_count, block_len),
            precision=EXACT,
        )
        mixing = jnp.einsum("tb,bnm->tnm", mask_now, per_block, precision=EXACT)
        change = jnp.einsum("tnm,nti->mti", mixing, deviation, precision=EXACT).reshape(
            members, cell_count
        )
        ensemble = ensemble + change
    return ensemble

def local(*arrays):
    state, obs_value, _, _, _, _, _, loc_mask = arrays
    per = obs_value.shape[1]
    owners, mem_devices = lax.axis_size("cols"), lax.axis_size("mem")
    tiles, batches, blocks = loc_mask.shape
    fits = (
        mem_devices == 4
        and owners == blocks == 8
        and per == LANES
        and batches == 4
        and tiles == 16
        and state.shape == (20, 64 * 512)
    )
    return fast(*arrays) if fits else plain(*arrays)


def solution(mesh):
    return jax.shard_map(
        local,
        mesh=mesh,
        in_specs=(
            P("mem", "cols"),
            P(None, "cols"),
            P(None, "cols"),
            P(None, "cols", None),
            P(None, "cols"),
            P(None, "cols", None),
            P(None, "cols"),
            P(("cols", "mem"), None, None),
        ),
        out_specs=P(None, ("cols", "mem")),
        check_vma=False,
    )
```

```python
import functools

import jax
import jax.numpy as jnp
from jax import lax
from jax.experimental import pallas as pl
from jax.experimental.pallas import tpu as pltpu
from jax.sharding import PartitionSpec as P

epsilon = 1e-05
EXACT = lax.Precision.HIGHEST
f32, bf16, i32 = jnp.float32, jnp.bfloat16, jnp.int32
LANES = 128
CHUNK = 256
TILE = 512
PAD = 24
WHOLE = pl.BlockSpec()
FAR = pl.BlockSpec(memory_space=pltpu.HBM)
PARAMS = pltpu.CompilerParams(vmem_limit_bytes=48 * 1024 * 1024)
ALONE = pltpu.CompilerParams(vmem_limit_bytes=64 * 1024 * 1024)


def cost(amount):
    return pl.CostEstimate(flops=0, bytes_accessed=amount, transcendentals=0)


def iota(shape, axis):
    return lax.broadcasted_iota(i32, shape, axis)


def dot(a, b, dims):
    return lax.dot_general(a, b, ((dims[0], dims[1]), ((), ())), preferred_element_type=f32)


def two(x):
    high = x.astype(bf16)
    return high, (x - high.astype(f32)).astype(bf16)


def slot_rows(sid, slots):
    return jnp.where(iota((slots, sid.shape[1]), 0) == sid, 1.0, 0.0).astype(bf16)


def route_kernel(owners, slots_per, *refs):
    ins, (msg_ref, sid_ref, table_ref), here, sems = refs[0:7], refs[7:10], refs[10:17], refs[17]
    copies = [pltpu.make_async_copy(a, b, sems.at[i]) for i, (a, b) in enumerate(zip(ins, here))]
    for copy in copies:
        copy.start()
    for copy in copies:
        copy.wait()
    owner_ref, tile_ref, off_ref, val_ref, var_ref, acc_ref, mask_ref = here
    batches, _, per = owner_ref.shape
    slots = owners * slots_per
    hot = [
        jnp.where(iota((owners, per), 0) == owner_ref[b], 1.0, 0.0) for b in range(batches)
    ]
    before = jnp.where(iota((per, per), 0) < iota((per, per), 1), 1.0, 0.0).astype(bf16)
    counts = dot(jnp.concatenate(hot, axis=0).astype(bf16), before, ((1,), (0,)))
    used = jnp.zeros((owners, 1), f32)
    total = jnp.zeros((16, slots), f32)
    for b in range(batches):
        own = owner_ref[b]
        rank = used + counts[b * owners : (b + 1) * owners]
        rank = jnp.sum(hot[b] * rank, axis=0, keepdims=True)
        used = used + jnp.sum(hot[b], axis=1, keepdims=True)
        sid = own * slots_per + rank.astype(i32)
        sid_ref[b : b + 1, :] = sid
        cells = tile_ref[b : b + 1, :] * 512 + off_ref[b]
        fields = jnp.concatenate(
            [(cells >> 7).astype(f32), (cells & 127).astype(f32), jnp.ones((8, per), f32)], axis=0
        ).astype(bf16)
        total = total + dot(fields, slot_rows(sid, slots), ((1,), (1,)))
    cells = total[0:4] * 128.0 + total[4:8] + (total[8:12] - 1.0)
    tiles = mask_ref.shape[1]
    kinds = mask_ref.shape[0]
    spread_out = jnp.where(iota((kinds, LANES), 0) == (iota((kinds, LANES), 1) & (kinds - 1)), 1.0, 0.0)
    wide = dot(mask_ref[...].astype(bf16), spread_out.astype(bf16), ((0,), (0,)))
    group = LANES // kinds
    lane_tile = iota((tiles, LANES), 1) // kinds
    for r in range(tiles // group):
        here = iota((tiles, LANES), 0) == lane_tile + r * group
        table_ref[r : r + 1, :] = jnp.sum(jnp.where(here, wide, 0.0), axis=0, keepdims=True)
    owner = jnp.concatenate([owner_ref[b] for b in range(batches)], axis=0)
    where_tile = (owner * 64 + tile_ref[...]).astype(f32)
    shared = jnp.concatenate(
        [val_ref[...], var_ref[...], acc_ref[...].astype(f32), where_tile], axis=0
    )
    for c in range(owners):
        msg_ref[c, 0:4, :] = cells[:, c * slots_per : (c + 1) * slots_per]
        msg_ref[c, 4:20, :] = shared


def cut_kernel(cuts, state_ref, *refs):
    sends, sem = refs[:-1], refs[-1]
    cells = state_ref.shape[1] // 4
    mem = lax.axis_index("mem")
    copies = []
    for ref, (k, begin, end) in zip(sends, cuts):
        start = pl.multiple_of((mem ^ k) * cells + begin, LANES)
        copies.append(pltpu.make_async_copy(state_ref.at[:, pl.ds(start, end - begin)], ref, sem.at[len(copies)]))
        copies[-1].start()
    for copy in copies:
        copy.wait()


def prepare_kernel(state_ref, out_ref):
    rows = state_ref.shape[0]
    fill = jnp.zeros((PAD - rows, TILE), f32)
    for t in range(state_ref.shape[1] // TILE):
        tile = jnp.concatenate([state_ref[:, t * TILE : (t + 1) * TILE], fill], axis=0)
        high = tile.astype(bf16).astype(f32)
        out_ref[t * 2 * PAD : (t + 1) * 2 * PAD, :] = jnp.concatenate([high, tile - high], axis=0).astype(bf16)


def pick_kernel(rows, msg_ref, parts_ref, out_ref, weight_ref):
    homes, _, slots_per = msg_ref.shape
    tiles = parts_ref.shape[0] // (2 * PAD)
    each = CHUNK // slots_per
    for g in range(homes // each):
        cells = jnp.concatenate([msg_ref[g * each + i, 0:4, :] for i in range(each)], axis=1)
        cells = jnp.maximum(cells.astype(i32), 0)
        weight = jnp.zeros((TILE, CHUNK), f32)
        for p in range(4):
            weight = weight + jnp.where(iota((TILE, CHUNK), 0) == (cells[p : p + 1] & (TILE - 1)), 0.25, 0.0)
        weight_ref[...] = weight.astype(bf16)
        tile = cells[0:1] >> 9
        sums = dot(parts_ref[...], weight_ref[...], ((1,), (0,)))
        total = jnp.zeros((PAD, CHUNK), f32)
        for t in range(tiles):
            both = sums[t * 2 * PAD : t * 2 * PAD + PAD] + sums[t * 2 * PAD + PAD : (t + 1) * 2 * PAD]
            total = total + jnp.where(tile == t, both, 0.0)
        for i in range(each):
            out_ref[g * each + i] = total[0:rows, i * slots_per : (i + 1) * slots_per]


def place_kernel(got_ref, sid_ref, table_ref, out_ref):
    owners, rows, slots_per = got_ref.shape
    batches, per = sid_ref.shape
    slots = owners * slots_per
    fill = jnp.zeros((PAD - rows, slots), f32)
    got = jnp.concatenate([got_ref[c] for c in range(owners)], axis=1)
    got = jnp.concatenate([got, fill], axis=0)
    first = got.astype(bf16).astype(f32)
    rest = got - first
    second = rest.astype(bf16).astype(f32)
    parts = jnp.concatenate([first, second, rest - second], axis=0).astype(bf16)
    for b in range(batches):
        out = dot(parts, slot_rows(sid_ref[b : b + 1, :], slots), ((1,), (0,)))
        out = out[0:PAD] + out[PAD : 2 * PAD] + out[2 * PAD : 3 * PAD]
        for c in range(owners):
            out_ref[c, b * rows : (b + 1) * rows, :] = out[0:rows]
    for c in range(owners):
        out_ref[c, batches * rows :, :] = table_ref[...]


def fill_masks(tiles, members, kinds, info_ref, table, mask_ref):
    homes = info_ref.shape[0]
    mem = lax.axis_index("mem")
    device = lax.axis_index("cols") * lax.axis_size("mem") + mem
    obs_chunks = 4 * homes // 2
    for idx in range(homes // 2, mask_ref.shape[0]):
        if idx < obs_chunks:
            b, h = idx // 4, 2 * (idx % 4)
            where_tile = jnp.concatenate([info_ref[h, 16 + b : 17 + b, :], info_ref[h + 1, 16 + b : 17 + b, :]], axis=1)
            where_tile = where_tile.astype(i32)
        else:
            column = iota((1, CHUNK), 1) + (idx - obs_chunks) * CHUNK
            where_tile = jnp.zeros((1, CHUNK), i32) + device * tiles
            for t in range(1, tiles):
                where_tile = where_tile + jnp.where(column >= t * members, 1, 0)
        row = ((((where_tile >> 4) & 3) ^ mem) * homes + (where_tile >> 6)) * 4 + ((where_tile >> 2) & 3)
        hot = jnp.where(iota((LANES, CHUNK), 0) == row, 1.0, 0.0).astype(bf16)
        rows = dot(table, hot, ((0,), (0,)))
        out = jnp.zeros((kinds, CHUNK), f32)
        for g in range(LANES // kinds):
            out = out + jnp.where((where_tile & 3) == g, rows[g * kinds : (g + 1) * kinds], 0.0)
        mask_ref[idx] = out


def split_kernel(*refs):
    state, near, pieces, out_ref = refs[0], refs[1], refs[2:-1], refs[-1]
    rows, total = near.shape
    here = pl.multiple_of(lax.axis_index("mem") * total, total)
    begin = 0
    for i in range(0, len(pieces), 2):
        end = begin + pieces[i].shape[1]
        cells = slice(begin, end)
        own = state[:, pl.ds(here + begin, end - begin)]
        whole = jnp.concatenate([own, near[:, cells], pieces[i][...], pieces[i + 1][...]], axis=0)
        high, low = two(whole)
        out_ref[0 : 4 * rows, cells] = high
        out_ref[4 * rows : 8 * rows, cells] = low
        begin = end


def window_kernel(tiles, rows, a_ref, b_ref, c_ref, d_ref, info_ref, ens_ref, out_ref, y_ref, w_ref, mask_ref):
    homes, all_rows, per = a_ref.shape
    batches = 4
    members = 4 * rows
    table = [ref[h, batches * rows :, :] for ref in (a_ref, b_ref, c_ref, d_ref) for h in range(homes)]
    table = jnp.concatenate(table, axis=0).astype(bf16)
    fill_masks(tiles, members, mask_ref.shape[1], info_ref, table, mask_ref)
    blocks = homes
    mem = lax.axis_index("mem")
    obs_chunks = batches * homes * per // CHUNK
    x_chunks = tiles * members // CHUNK
    for b in range(batches):
        for h in range(homes):
            chunk, place = b * (homes // 2) + h // 2, (h % 2) * per
            y_ref[chunk, :, place : place + per] = jnp.concatenate(
                [ref[h, b * rows : (b + 1) * rows, :] for ref in (a_ref, b_ref, c_ref, d_ref)], axis=0
            )
    member = iota((members, CHUNK), 0)
    for q in range(x_chunks):
        column = iota((1, CHUNK), 1) + q * CHUNK
        tile = jnp.zeros((1, CHUNK), i32)
        for t in range(1, tiles):
            tile = tile + jnp.where(column >= t * members, 1, 0)
        y_ref[obs_chunks + q] = jnp.where(member == column - tile * members, 1.0, 0.0)

    lane3 = iota((members, 3 * members), 1)
    for b in range(batches):
        for g in range(homes // 2):
            def field(f):
                return jnp.concatenate(
                    [info_ref[h, 4 + 4 * f + b : 5 + 4 * f + b, :] for h in (2 * g, 2 * g + 1)], axis=1
                )

            prior = y_ref[b * (homes // 2) + g]
            mean = jnp.sum(prior, axis=0, keepdims=True) / members
            spread = prior - mean
            var = jnp.sum(spread * spread, axis=0, keepdims=True) / (members - 1) + epsilon
            noise = field(1)
            denominator = var + noise
            shift = var / denominator * (field(0) - mean)
            factor = jnp.sqrt(noise / denominator) - 1.0
            increment = field(2) * (shift + factor * spread)
            scaled = spread / ((members - 1) * var)
            ih, il = two(increment)
            sh, sl = two(scaled)
            for i in range(2):
                lanes = slice(i * per, (i + 1) * per)
                left = jnp.concatenate([ih[:, lanes], ih[:, lanes], il[:, lanes]], axis=1)
                right = jnp.concatenate([sh[:, lanes], sl[:, lanes], sh[:, lanes]], axis=1)
                right = jnp.concatenate([right, right, right], axis=0)
                block = dot(left, right, ((1,), (1,)))
                high = block.astype(bf16).astype(f32)
                block = jnp.where(lane3 < 2 * members, high, block - high)
                h = 2 * g + i
                w_ref[h * members : (h + 1) * members, :] = block.astype(bf16)

        def update(idx, b=b):
            now = y_ref[idx]
            deviation = now - jnp.sum(now, axis=0, keepdims=True) / members
            dh, dl = two(deviation)
            moved = dot(w_ref[...], jnp.concatenate([dh, dl, dh], axis=0), ((1,), (0,)))
            for k in range(blocks):
                now = now + mask_ref[idx, b * blocks + k : b * blocks + k + 1, :] * moved[
                    k * members : (k + 1) * members
                ]
            y_ref[idx] = now

        for idx in range((b + 1) * (homes // 2), obs_chunks + x_chunks):
            update(idx)

    size = out_ref.shape[1] // tiles
    true, at = iota((members, members), 0), iota((members, members), 1)
    part = jnp.zeros((members, members), i32)
    for k in range(1, 4):
        part = part + jnp.where(at >= k * rows, 1, 0)
    order = jnp.where(true == at - part * rows + (part ^ mem) * rows, 1.0, 0.0)
    order = jnp.concatenate([order, order, order], axis=1).astype(bf16)
    flat = []
    for q in range(x_chunks):
        now = y_ref[obs_chunks + q]
        first = now.astype(bf16).astype(f32)
        rest = now - first
        second = rest.astype(bf16).astype(f32)
        stack = jnp.concatenate([first, second, rest - second], axis=0).astype(bf16)
        flat.append(dot(order, stack, ((1,), (0,))))
    flat = jnp.concatenate(flat, axis=1)
    for t in range(tiles):
        weight = flat[:, t * members : (t + 1) * members]
        high = weight.astype(bf16).astype(f32)
        weight = jnp.concatenate([high, high, weight - high], axis=1).astype(bf16)
        cells = slice(t * size, (t + 1) * size)
        ens_high, ens_low = ens_ref[0:members, cells], ens_ref[members : 2 * members, cells]
        out_ref[:, cells] = dot(weight, jnp.concatenate([ens_high, ens_low, ens_high], axis=0), ((1,), (0,)))


def window_call(tiles, rows, kinds, mine, by_core, by_x, by_both, about, pieces):
    owners, _, per = mine.shape
    members, cells = pieces.shape[0] // 2, pieces.shape[1]
    chunks = (4 * owners * per + tiles * members) // CHUNK
    return pl.pallas_call(
        functools.partial(window_kernel, tiles, rows),
        out_shape=jax.ShapeDtypeStruct((members, cells), f32),
        in_specs=[WHOLE] * 6,
        out_specs=WHOLE,
        scratch_shapes=[
            pltpu.VMEM((chunks, members, CHUNK), f32),
            pltpu.VMEM((owners * members, 3 * members), bf16),
            pltpu.VMEM((chunks, kinds, CHUNK), f32),
        ],
        compiler_params=PARAMS,
        name="window",
    )(mine, by_core, by_x, by_both, about, pieces)


def fast(state, obs_value, obs_var, owner, tile_of, offsets, accept, loc_mask):
    owners = lax.axis_size("cols")
    mem_devices = lax.axis_size("mem")
    mem = lax.axis_index("mem")
    batches, per = obs_value.shape
    rows, slab = state.shape
    members = rows * mem_devices
    cells = slab // mem_devices
    tiles = loc_mask.shape[0]
    kinds = loc_mask.shape[1] * loc_mask.shape[2]
    cap = 2 * per // owners
    slots_per = batches * cap

    about = (
        owner.transpose(0, 2, 1),
        tile_of,
        offsets.transpose(0, 2, 1),
        obs_value,
        obs_var,
        accept,
        loc_mask.transpose(1, 2, 0).reshape(kinds, tiles),
    )
    msg, sid, table = pl.pallas_call(
        functools.partial(route_kernel, owners, slots_per),
        out_shape=(
            jax.ShapeDtypeStruct((owners, 20, slots_per), f32),
            jax.ShapeDtypeStruct((batches, per), i32),
            jax.ShapeDtypeStruct((tiles * kinds // LANES, LANES), f32),
        ),
        in_specs=[FAR] * 7,
        out_specs=(WHOLE,) * 3,
        scratch_shapes=[pltpu.VMEM(a.shape, a.dtype) for a in about] + [pltpu.SemaphoreType.DMA((7,))],
        compiler_params=ALONE,
        name="route",
    )(*about)
    state, msg = lax.optimization_barrier((state, msg))
    arrived = lax.all_to_all(msg, "cols", split_axis=0, concat_axis=0, tiled=True)

    marks = [0, cells * 8 // 16, cells * 12 // 16, cells]
    cuts = [(1, 0, cells)] + [(k, marks[i], marks[i + 1]) for i in range(3) for k in (2, 3)]
    sends = pl.pallas_call(
        functools.partial(cut_kernel, cuts),
        out_shape=tuple(jax.ShapeDtypeStruct((rows, end - begin), f32) for _, begin, end in cuts),
        in_specs=[WHOLE],
        out_specs=(FAR,) * len(cuts),
        scratch_shapes=[pltpu.SemaphoreType.DMA((len(cuts),))],
        compiler_params=ALONE,
        cost_estimate=cost(1024),
        name="cut",
    )(state)
    parts = pl.pallas_call(
        prepare_kernel,
        out_shape=jax.ShapeDtypeStruct((slab // TILE * 2 * PAD, TILE), bf16),
        in_specs=[WHOLE],
        out_specs=WHOLE,
        compiler_params=PARAMS,
        cost_estimate=cost(1024),
        name="prepare",
    )(state)

    def swap(array, k):
        return lax.ppermute(array, "mem", [(i, i ^ k) for i in range(4)])

    far = [swap(array, k) for array, (k, _, _) in zip(sends[1:], cuts[1:])]
    first, second, third = far[0:2], far[2:4], far[4:6]
    priors = pl.pallas_call(
        functools.partial(pick_kernel, rows),
        out_shape=jax.ShapeDtypeStruct((owners, rows, slots_per), f32),
        in_specs=[WHOLE] * 2,
        out_specs=WHOLE,
        scratch_shapes=[pltpu.VMEM((TILE, CHUNK), bf16)],
        compiler_params=PARAMS,
        cost_estimate=cost(1024),
        name="pick",
    )(arrived, parts)
    at_home = lax.all_to_all(priors, "cols", split_axis=0, concat_axis=0, tiled=True)
    at_home, *first = lax.optimization_barrier((at_home, *first))
    everyone = pl.pallas_call(
        place_kernel,
        out_shape=jax.ShapeDtypeStruct((owners, batches * rows + table.shape[0], per), f32),
        in_specs=[WHOLE] * 3,
        out_specs=WHOLE,
        compiler_params=PARAMS,
        name="place",
    )(at_home, sid, table)
    everyone, near, *second = lax.optimization_barrier((everyone, sends[0], *second))
    near = swap(near, 1)
    mine = lax.all_to_all(everyone, "cols", split_axis=0, concat_axis=0, tiled=True)
    mine, *third = lax.optimization_barrier((mine, *third))
    pieces = pl.pallas_call(
        split_kernel,
        out_shape=jax.ShapeDtypeStruct((2 * members, cells), bf16),
        in_specs=[WHOLE] * 8,
        out_specs=WHOLE,
        compiler_params=PARAMS,
        name="split",
    )(state, near, *first, *second, *third)
    by_core, by_x = swap(mine, 1), swap(mine, 2)
    by_x, pieces = lax.optimization_barrier((by_x, pieces))
    by_both = swap(by_x, 1)
    return window_call(tiles, rows, kinds, mine, by_core, by_x, by_both, arrived, pieces)


def innovations(prior_obs, observed, obs_noise, accepted):
    members = prior_obs.shape[0]
    mean_prior = jnp.mean(prior_obs, axis=0)
    spread = prior_obs - mean_prior
    spread_var = jnp.sum(spread * spread, axis=0) / (members - 1) + epsilon
    denominator = spread_var + obs_noise
    mean_shift = spread_var / denominator * (observed - mean_prior)
    factor = jnp.sqrt(obs_noise / denominator) - 1.0
    increment = accepted * (mean_shift + factor * spread)
    scaled = spread / ((members - 1) * spread_var)
    return (increment, scaled)


def plain(state, obs_value, obs_var, owner, tile_of, offsets, accept, loc_mask):
    col_devices = lax.axis_size("cols")
    mem_devices = lax.axis_size("mem")
    source = lax.axis_index("cols")
    mem_index = lax.axis_index("mem")
    batch_total, per_src = obs_value.shape
    pick_count = offsets.shape[2]
    members = state.shape[0] * mem_devices
    cell_count = state.shape[1] // mem_devices
    tiles_here = loc_mask.shape[0]
    tile_len = cell_count // tiles_here
    block_count = loc_mask.shape[2]
    batch_obs = per_src * col_devices
    block_len = batch_obs // block_count
    capacity = max(2, 2 * per_src // col_devices)
    slot_count = col_devices * capacity
    destination = owner[:, :, 0]
    ordinal = jnp.arange(per_src, dtype=jnp.int32)
    same_owner = destination[:, :, None] == destination[:, None, :]
    earlier = (ordinal[None, :] < ordinal[:, None])[None]
    slot_rank = jnp.sum((same_owner & earlier).astype(jnp.int32), axis=2)
    batch_rows = jnp.broadcast_to(
        jnp.arange(batch_total, dtype=jnp.int32)[:, None], destination.shape
    )
    position = jnp.broadcast_to(source * per_src + ordinal, destination.shape)
    fields = jnp.concatenate(
        [tile_of[:, :, None], accept[:, :, None], position[:, :, None], offsets], axis=2
    )
    blank_int = (
        jnp.zeros((batch_total, col_devices, capacity, 3 + pick_count), jnp.int32)
        .at[:, :, :, 2]
        .set(-1)
    )
    sent_int = blank_int.at[batch_rows, destination, slot_rank].set(fields)
    blank_val = (
        jnp.zeros((batch_total, col_devices, capacity, 2), jnp.float32).at[:, :, :, 1].set(1.0)
    )
    sent_val = blank_val.at[batch_rows, destination, slot_rank].set(
        jnp.stack([obs_value, obs_var], axis=2)
    )
    arrived_int = lax.all_to_all(sent_int, "cols", split_axis=1, concat_axis=1, tiled=True).reshape(
        batch_total, slot_count, 3 + pick_count
    )
    arrived_val = lax.all_to_all(sent_val, "cols", split_axis=1, concat_axis=1, tiled=True).reshape(
        batch_total, slot_count, 2
    )
    obs_tile = arrived_int[:, :, 0]
    obs_flag = arrived_int[:, :, 1].astype(jnp.float32)
    obs_pos = arrived_int[:, :, 2]
    obs_off = arrived_int[:, :, 3:]
    observed = arrived_val[:, :, 0]
    obs_noise = arrived_val[:, :, 1]
    targets = jnp.where(obs_pos >= 0, obs_pos, batch_obs)
    ensemble = lax.all_to_all(state, "mem", split_axis=1, concat_axis=0, tiled=True)
    for batch_no in range(batch_total):
        local_cell = (
            obs_tile[batch_no][:, None] * tile_len + obs_off[batch_no] - mem_index * cell_count
        )
        inside = (local_cell >= 0) & (local_cell < cell_count) & (obs_pos[batch_no] >= 0)[:, None]
        flat_cells = jnp.clip(local_cell, 0, cell_count - 1).reshape(-1)
        picked = jnp.take(ensemble, flat_cells, axis=1).reshape(members, slot_count, pick_count)
        prior_obs = lax.psum(
            jnp.sum(jnp.where(inside[None], picked, 0.0), axis=2) / pick_count, "mem"
        )
        increment, scaled = innovations(
            prior_obs, observed[batch_no], obs_noise[batch_no], obs_flag[batch_no]
        )
        blank_panel = jnp.zeros((members, batch_obs), jnp.float32)
        placed_inc = blank_panel.at[:, targets[batch_no]].add(increment, mode="drop")
        placed_scl = blank_panel.at[:, targets[batch_no]].add(scaled, mode="drop")
        inc_all, scl_all = lax.psum((placed_inc, placed_scl), "cols")
        mask_now = loc_mask[:, batch_no, :].astype(jnp.float32)
        mean_state = jnp.mean(ensemble, axis=0)
        deviation = (ensemble - mean_state).reshape(members, tiles_here, tile_len)
        per_block = jnp.einsum(
            "nbk,mbk->bnm",
            scl_all.reshape(members, block_count, block_len),
            inc_all.reshape(members, block_count, block_len),
            precision=EXACT,
        )
        mixing = jnp.einsum("tb,bnm->tnm", mask_now, per_block, precision=EXACT)
        change = jnp.einsum("tnm,nti->mti", mixing, deviation, precision=EXACT).reshape(
            members, cell_count
        )
        ensemble = ensemble + change
    return ensemble

def local(*arrays):
    state, obs_value, _, _, _, _, _, loc_mask = arrays
    per = obs_value.shape[1]
    owners, mem_devices = lax.axis_size("cols"), lax.axis_size("mem")
    tiles, batches, blocks = loc_mask.shape
    fits = (
        mem_devices == 4
        and owners == blocks == 8
        and per == LANES
        and batches == 4
        and tiles == 16
        and state.shape == (20, 64 * 512)
    )
    return fast(*arrays) if fits else plain(*arrays)


def solution(mesh):
    return jax.shard_map(
        local,
        mesh=mesh,
        in_specs=(
            P("mem", "cols"),
            P(None, "cols"),
            P(None, "cols"),
            P(None, "cols", None),
            P(None, "cols"),
            P(None, "cols", None),
            P(None, "cols"),
            P(("cols", "mem"), None, None),
        ),
        out_specs=P(None, ("cols", "mem")),
        check_vma=False,
    )
```

```python
import functools

import jax
import jax.numpy as jnp
from jax import lax
from jax.experimental import pallas as pl
from jax.experimental.pallas import tpu as pltpu
from jax.sharding import PartitionSpec as P

epsilon = 1e-05
EXACT = lax.Precision.HIGHEST
f32, bf16, i32 = jnp.float32, jnp.bfloat16, jnp.int32
LANES = 128
CHUNK = 256
TILE = 512
SWAPS = ((2, 0, 8), (3, 0, 8), (2, 8, 13), (3, 8, 13), (2, 13, 16), (3, 13, 16))
PAD = 24
WHOLE = pl.BlockSpec()
FAR = pl.BlockSpec(memory_space=pltpu.HBM)
PARAMS = pltpu.CompilerParams(vmem_limit_bytes=48 * 1024 * 1024)
ALONE = pltpu.CompilerParams(vmem_limit_bytes=64 * 1024 * 1024)
NEARLY = pltpu.CompilerParams(vmem_limit_bytes=64 * 1024 * 1024 - 200 * 1024)


def cost(amount):
    return pl.CostEstimate(flops=0, bytes_accessed=amount, transcendentals=0)


def iota(shape, axis):
    return lax.broadcasted_iota(i32, shape, axis)


def dot(a, b, dims):
    return lax.dot_general(a, b, ((dims[0], dims[1]), ((), ())), preferred_element_type=f32)


def two(x):
    high = x.astype(bf16)
    return high, (x - high.astype(f32)).astype(bf16)


def slot_rows(sid, slots):
    return jnp.where(iota((slots, sid.shape[1]), 0) == sid, 1.0, 0.0).astype(bf16)


def route_kernel(owners, slots_per, cuts, *refs):
    n = len(cuts)
    ins, state_ref, (msg_ref, sid_ref) = refs[0:7], refs[7], refs[8:10]
    sends, here, held, sems = refs[10 : 10 + n], refs[10 + n : 17 + n], refs[17 + n : 17 + 2 * n], refs[17 + 2 * n]
    cells = state_ref.shape[1] // 4
    mem = lax.axis_index("mem")
    copies = [pltpu.make_async_copy(a, b, sems.at[i]) for i, (a, b) in enumerate(zip(ins, here))]
    for copy in copies:
        copy.start()
    cutting = []
    for i, (k, begin, end) in enumerate(cuts):
        start = pl.multiple_of((mem ^ k) * cells + begin, LANES)
        cutting.append(pltpu.make_async_copy(state_ref.at[:, pl.ds(start, end - begin)], held[i], sems.at[7 + i]))
        cutting[-1].start()
    for copy in copies:
        copy.wait()
    for copy in cutting:
        copy.wait()
    sending = [pltpu.make_async_copy(held[i], sends[i], sems.at[7 + n + i]) for i in range(n)]
    for copy in sending:
        copy.start()
    owner_ref, tile_ref, off_ref, val_ref, var_ref, acc_ref, mask_ref = here
    batches, _, per = owner_ref.shape
    slots = owners * slots_per
    hot = [
        jnp.where(iota((owners, per), 0) == owner_ref[b], 1.0, 0.0) for b in range(batches)
    ]
    before = jnp.where(iota((per, per), 0) < iota((per, per), 1), 1.0, 0.0).astype(bf16)
    counts = dot(jnp.concatenate(hot, axis=0).astype(bf16), before, ((1,), (0,)))
    used = jnp.zeros((owners, 1), f32)
    total = jnp.zeros((16, slots), f32)
    for b in range(batches):
        own = owner_ref[b]
        rank = used + counts[b * owners : (b + 1) * owners]
        rank = jnp.sum(hot[b] * rank, axis=0, keepdims=True)
        used = used + jnp.sum(hot[b], axis=1, keepdims=True)
        sid = own * slots_per + rank.astype(i32)
        sid_ref[b : b + 1, :] = sid
        cells = tile_ref[b : b + 1, :] * 512 + off_ref[b]
        fields = jnp.concatenate(
            [(cells >> 7).astype(f32), (cells & 127).astype(f32), jnp.ones((8, per), f32)], axis=0
        ).astype(bf16)
        total = total + dot(fields, slot_rows(sid, slots), ((1,), (1,)))
    where = total[0:4] * 128.0 + total[4:8] + (total[8:12] - 1.0)
    tiles = mask_ref.shape[1]
    kinds = mask_ref.shape[0]
    spread_out = jnp.where(iota((kinds, LANES), 0) == (iota((kinds, LANES), 1) & (kinds - 1)), 1.0, 0.0)
    wide = dot(mask_ref[...].astype(bf16), spread_out.astype(bf16), ((0,), (0,)))
    group = LANES // kinds
    lane_tile = iota((tiles, LANES), 1) // kinds
    table = [
        jnp.sum(jnp.where(iota((tiles, LANES), 0) == lane_tile + r * group, wide, 0.0), axis=0, keepdims=True)
        for r in range(tiles // group)
    ]
    owner = jnp.concatenate([owner_ref[b] for b in range(batches)], axis=0)
    where_tile = (owner * 64 + tile_ref[...]).astype(f32)
    shared = jnp.concatenate(
        [val_ref[...], var_ref[...], acc_ref[...].astype(f32), where_tile] + table, axis=0
    )
    for c in range(owners):
        msg_ref[c, 0:4, :] = where[:, c * slots_per : (c + 1) * slots_per]
        msg_ref[c, 4:24, :] = shared
    for copy in sending:
        copy.wait()


def cut_kernel(cuts, state_ref, *refs):
    sends, sem = refs[:-1], refs[-1]
    cells = state_ref.shape[1] // 4
    mem = lax.axis_index("mem")
    copies = []
    for ref, (k, begin, end) in zip(sends, cuts):
        start = pl.multiple_of((mem ^ k) * cells + begin, LANES)
        copies.append(pltpu.make_async_copy(state_ref.at[:, pl.ds(start, end - begin)], ref, sem.at[len(copies)]))
        copies[-1].start()
    for copy in copies:
        copy.wait()


def prepare_kernel(state_ref, out_ref):
    rows = state_ref.shape[0]
    fill = jnp.zeros((PAD - rows, TILE), f32)
    for t in range(state_ref.shape[1] // TILE):
        tile = jnp.concatenate([state_ref[:, t * TILE : (t + 1) * TILE], fill], axis=0)
        high = tile.astype(bf16).astype(f32)
        out_ref[t * 2 * PAD : (t + 1) * 2 * PAD, :] = jnp.concatenate([high, tile - high], axis=0).astype(bf16)


def pick_kernel(rows, msg_ref, parts_ref, out_ref, table_ref, weight_ref):
    homes, _, slots_per = msg_ref.shape
    tiles = parts_ref.shape[0] // (2 * PAD)
    each = CHUNK // slots_per
    table_ref[...] = msg_ref[:, 20:24, :]
    for g in range(homes // each):
        cells = jnp.concatenate([msg_ref[g * each + i, 0:4, :] for i in range(each)], axis=1)
        cells = jnp.maximum(cells.astype(i32), 0)
        weight = jnp.zeros((TILE, CHUNK), f32)
        for p in range(4):
            weight = weight + jnp.where(iota((TILE, CHUNK), 0) == (cells[p : p + 1] & (TILE - 1)), 0.25, 0.0)
        weight_ref[...] = weight.astype(bf16)
        tile = cells[0:1] >> 9
        sums = dot(parts_ref[...], weight_ref[...], ((1,), (0,)))
        total = jnp.zeros((PAD, CHUNK), f32)
        for t in range(tiles):
            both = sums[t * 2 * PAD : t * 2 * PAD + PAD] + sums[t * 2 * PAD + PAD : (t + 1) * 2 * PAD]
            total = total + jnp.where(tile == t, both, 0.0)
        for i in range(each):
            out_ref[g * each + i] = total[0:rows, i * slots_per : (i + 1) * slots_per]


def place_kernel(got_ref, sid_ref, out_ref):
    owners, rows, slots_per = got_ref.shape
    batches, per = sid_ref.shape
    slots = owners * slots_per
    fill = jnp.zeros((PAD - rows, slots), f32)
    got = jnp.concatenate([got_ref[c] for c in range(owners)], axis=1)
    got = jnp.concatenate([got, fill], axis=0)
    first = got.astype(bf16).astype(f32)
    rest = got - first
    second = rest.astype(bf16).astype(f32)
    parts = jnp.concatenate([first, second, rest - second], axis=0).astype(bf16)
    for b in range(batches):
        out = dot(parts, slot_rows(sid_ref[b : b + 1, :], slots), ((1,), (0,)))
        out = out[0:PAD] + out[PAD : 2 * PAD] + out[2 * PAD : 3 * PAD]
        for c in range(owners):
            out_ref[c, b * rows : (b + 1) * rows, :] = out[0:rows]


def fill_masks(tiles, members, kinds, info_ref, table, mask_ref):
    homes = info_ref.shape[0]
    mem = lax.axis_index("mem")
    device = lax.axis_index("cols") * lax.axis_size("mem") + mem
    obs_chunks = 4 * homes // 2
    for idx in range(homes // 2, mask_ref.shape[0]):
        if idx < obs_chunks:
            b, h = idx // 4, 2 * (idx % 4)
            where_tile = jnp.concatenate([info_ref[h, 16 + b : 17 + b, :], info_ref[h + 1, 16 + b : 17 + b, :]], axis=1)
            where_tile = where_tile.astype(i32)
        else:
            column = iota((1, CHUNK), 1) + (idx - obs_chunks) * CHUNK
            where_tile = jnp.zeros((1, CHUNK), i32) + device * tiles
            for t in range(1, tiles):
                where_tile = where_tile + jnp.where(column >= t * members, 1, 0)
        row = ((((where_tile >> 4) & 3) ^ mem) * homes + (where_tile >> 6)) * 4 + ((where_tile >> 2) & 3)
        hot = jnp.where(iota((LANES, CHUNK), 0) == row, 1.0, 0.0).astype(bf16)
        rows = dot(table, hot, ((0,), (0,)))
        out = jnp.zeros((kinds, CHUNK), f32)
        for g in range(LANES // kinds):
            out = out + jnp.where((where_tile & 3) == g, rows[g * kinds : (g + 1) * kinds], 0.0)
        mask_ref[idx] = out


def split_kernel(cuts, *refs):
    state, received, out_ref = refs[0], refs[1:-1], refs[-1]
    rows, total = received[0].shape
    here = pl.multiple_of(lax.axis_index("mem") * total, total)
    marks = sorted({cut[1] for cut in cuts} | {cut[2] for cut in cuts})
    for begin, end in zip(marks[:-1], marks[1:]):
        parts = [state[:, pl.ds(here + begin, end - begin)]]
        for k in (1, 2, 3):
            for ref, (to, first, last) in zip(received, cuts):
                if to == k and first <= begin and end <= last:
                    parts.append(ref[:, begin - first : end - first])
        high, low = two(jnp.concatenate(parts, axis=0))
        out_ref[0 : 4 * rows, begin:end] = high
        out_ref[4 * rows : 8 * rows, begin:end] = low


def mask_kernel(tiles, rows, info_ref, a_ref, b_ref, c_ref, d_ref, mask_ref):
    homes = info_ref.shape[0]
    table = [ref[h] for ref in (a_ref, b_ref, c_ref, d_ref) for h in range(homes)]
    table = jnp.concatenate(table, axis=0).astype(bf16)
    fill_masks(tiles, 4 * rows, mask_ref.shape[1], info_ref, table, mask_ref)


def window_kernel(tiles, rows, a_ref, b_ref, c_ref, d_ref, info_ref, mask_ref, ens_ref, out_ref, y_ref, w_ref, held_ref, sem):
    homes, all_rows, per = a_ref.shape
    batches = 4
    members = 4 * rows
    blocks = homes
    mem = lax.axis_index("mem")
    obs_chunks = batches * homes * per // CHUNK
    x_chunks = tiles * members // CHUNK
    for b in range(batches):
        for h in range(homes):
            chunk, place = b * (homes // 2) + h // 2, (h % 2) * per
            y_ref[chunk, :, place : place + per] = jnp.concatenate(
                [ref[h, b * rows : (b + 1) * rows, :] for ref in (a_ref, b_ref, c_ref, d_ref)], axis=0
            )
    member = iota((members, CHUNK), 0)
    for q in range(x_chunks):
        column = iota((1, CHUNK), 1) + q * CHUNK
        tile = jnp.zeros((1, CHUNK), i32)
        for t in range(1, tiles):
            tile = tile + jnp.where(column >= t * members, 1, 0)
        y_ref[obs_chunks + q] = jnp.where(member == column - tile * members, 1.0, 0.0)

    lane3 = iota((members, 3 * members), 1)
    for b in range(batches):
        for g in range(homes // 2):
            def field(f):
                return jnp.concatenate(
                    [info_ref[h, 4 + 4 * f + b : 5 + 4 * f + b, :] for h in (2 * g, 2 * g + 1)], axis=1
                )

            prior = y_ref[b * (homes // 2) + g]
            mean = jnp.sum(prior, axis=0, keepdims=True) / members
            spread = prior - mean
            var = jnp.sum(spread * spread, axis=0, keepdims=True) / (members - 1) + epsilon
            noise = field(1)
            denominator = var + noise
            shift = var / denominator * (field(0) - mean)
            factor = jnp.sqrt(noise / denominator) - 1.0
            increment = field(2) * (shift + factor * spread)
            scaled = spread / ((members - 1) * var)
            ih, il = two(increment)
            sh, sl = two(scaled)
            for i in range(2):
                lanes = slice(i * per, (i + 1) * per)
                left = jnp.concatenate([ih[:, lanes], ih[:, lanes], il[:, lanes]], axis=1)
                right = jnp.concatenate([sh[:, lanes], sl[:, lanes], sh[:, lanes]], axis=1)
                right = jnp.concatenate([right, right, right], axis=0)
                block = dot(left, right, ((1,), (1,)))
                high = block.astype(bf16).astype(f32)
                block = jnp.where(lane3 < 2 * members, high, block - high)
                h = 2 * g + i
                w_ref[h * members : (h + 1) * members, :] = block.astype(bf16)

        def update(idx, b=b):
            now = y_ref[idx]
            deviation = now - jnp.sum(now, axis=0, keepdims=True) / members
            dh, dl = two(deviation)
            moved = dot(w_ref[...], jnp.concatenate([dh, dl, dh], axis=0), ((1,), (0,)))
            for k in range(blocks):
                now = now + mask_ref[idx, b * blocks + k : b * blocks + k + 1, :] * moved[
                    k * members : (k + 1) * members
                ]
            y_ref[idx] = now

        for idx in range((b + 1) * (homes // 2), obs_chunks + x_chunks):
            update(idx)

    size = out_ref.shape[1] // tiles
    true, at = iota((members, members), 0), iota((members, members), 1)
    part = jnp.zeros((members, members), i32)
    for k in range(1, 4):
        part = part + jnp.where(at >= k * rows, 1, 0)
    order = jnp.where(true == at - part * rows + (part ^ mem) * rows, 1.0, 0.0)
    order = jnp.concatenate([order, order, order], axis=1).astype(bf16)
    flat = []
    for q in range(x_chunks):
        now = y_ref[obs_chunks + q]
        first = now.astype(bf16).astype(f32)
        rest = now - first
        second = rest.astype(bf16).astype(f32)
        stack = jnp.concatenate([first, second, rest - second], axis=0).astype(bf16)
        flat.append(dot(order, stack, ((1,), (0,))))
    flat = jnp.concatenate(flat, axis=1)
    copies = []
    for t in range(tiles):
        weight = flat[:, t * members : (t + 1) * members]
        high = weight.astype(bf16).astype(f32)
        weight = jnp.concatenate([high, high, weight - high], axis=1).astype(bf16)
        cells = slice(t * size, (t + 1) * size)
        ens_high, ens_low = ens_ref[0:members, cells], ens_ref[members : 2 * members, cells]
        held_ref[t] = dot(weight, jnp.concatenate([ens_high, ens_low, ens_high], axis=0), ((1,), (0,)))
        copies.append(pltpu.make_async_copy(held_ref.at[t], out_ref.at[:, cells], sem.at[t]))
        copies[-1].start()
    for copy in copies:
        copy.wait()


def window_call(tiles, rows, mine, by_core, by_x, by_both, about, masks, pieces):
    owners, _, per = mine.shape
    members, cells = pieces.shape[0] // 2, pieces.shape[1]
    chunks = masks.shape[0]
    return pl.pallas_call(
        functools.partial(window_kernel, tiles, rows),
        out_shape=jax.ShapeDtypeStruct((members, cells), f32),
        in_specs=[WHOLE] * 7,
        out_specs=FAR,
        scratch_shapes=[
            pltpu.VMEM((chunks, members, CHUNK), f32),
            pltpu.VMEM((owners * members, 3 * members), bf16),
            pltpu.VMEM((tiles, members, cells // tiles), f32),
            pltpu.SemaphoreType.DMA((tiles,)),
        ],
        compiler_params=PARAMS,
        name="window",
    )(mine, by_core, by_x, by_both, about, masks, pieces)


def fast(state, obs_value, obs_var, owner, tile_of, offsets, accept, loc_mask):
    owners = lax.axis_size("cols")
    mem_devices = lax.axis_size("mem")
    mem = lax.axis_index("mem")
    batches, per = obs_value.shape
    rows, slab = state.shape
    members = rows * mem_devices
    cells = slab // mem_devices
    tiles = loc_mask.shape[0]
    kinds = loc_mask.shape[1] * loc_mask.shape[2]
    cap = 2 * per // owners
    slots_per = batches * cap

    about = (
        owner.transpose(0, 2, 1),
        tile_of,
        offsets.transpose(0, 2, 1),
        obs_value,
        obs_var,
        accept,
        loc_mask.transpose(1, 2, 0).reshape(kinds, tiles),
    )
    cuts = [(1, 0, cells)] + [(k, cells * a // 16, cells * b // 16) for k, a, b in SWAPS]
    sooner, later = cuts[1:3], cuts[0:1] + cuts[3:]
    msg, sid, *first = pl.pallas_call(
        functools.partial(route_kernel, owners, slots_per, sooner),
        out_shape=(
            jax.ShapeDtypeStruct((owners, 24, slots_per), f32),
            jax.ShapeDtypeStruct((batches, per), i32),
            *(jax.ShapeDtypeStruct((rows, end - begin), f32) for _, begin, end in sooner),
        ),
        in_specs=[FAR] * 8,
        out_specs=(WHOLE,) * 2 + (FAR,) * len(sooner),
        scratch_shapes=[pltpu.VMEM(a.shape, a.dtype) for a in about]
        + [pltpu.VMEM((rows, end - begin), f32) for _, begin, end in sooner]
        + [pltpu.SemaphoreType.DMA((7 + 2 * len(sooner),))],
        compiler_params=ALONE,
        name="route",
    )(*about, state)
    state, msg = lax.optimization_barrier((state, msg))
    arrived = lax.all_to_all(msg, "cols", split_axis=0, concat_axis=0, tiled=True)

    sends = pl.pallas_call(
        functools.partial(cut_kernel, later),
        out_shape=tuple(jax.ShapeDtypeStruct((rows, end - begin), f32) for _, begin, end in later),
        in_specs=[WHOLE],
        out_specs=(FAR,) * len(later),
        scratch_shapes=[pltpu.SemaphoreType.DMA((len(later),))],
        compiler_params=NEARLY,
        cost_estimate=cost(1024),
        name="cut",
    )(state)
    parts = pl.pallas_call(
        prepare_kernel,
        out_shape=jax.ShapeDtypeStruct((slab // TILE * 2 * PAD, TILE), bf16),
        in_specs=[WHOLE],
        out_specs=WHOLE,
        compiler_params=PARAMS,
        cost_estimate=cost(1024),
        name="prepare",
    )(state)

    def swap(array, k):
        return lax.ppermute(array, "mem", [(i, i ^ k) for i in range(4)])

    first = [swap(array, k) for array, (k, _, _) in zip(first, sooner)]
    far = [swap(array, k) for array, (k, _, _) in zip(sends[1:], later[1:])]
    second, third = far[0:2], far[2:]
    priors, table = pl.pallas_call(
        functools.partial(pick_kernel, rows),
        out_shape=(
            jax.ShapeDtypeStruct((owners, rows, slots_per), f32),
            jax.ShapeDtypeStruct((owners, 4, LANES), f32),
        ),
        in_specs=[WHOLE] * 2,
        out_specs=(WHOLE,) * 2,
        scratch_shapes=[pltpu.VMEM((TILE, CHUNK), bf16)],
        compiler_params=PARAMS,
        cost_estimate=cost(1024),
        name="pick",
    )(arrived, parts)
    at_home = lax.all_to_all(priors, "cols", split_axis=0, concat_axis=0, tiled=True)
    at_home, *first = lax.optimization_barrier((at_home, *first))
    everyone = pl.pallas_call(
        place_kernel,
        out_shape=jax.ShapeDtypeStruct((owners, batches * rows, per), f32),
        in_specs=[WHOLE] * 2,
        out_specs=WHOLE,
        compiler_params=PARAMS,
        name="place",
    )(at_home, sid)
    everyone, near, table, *second = lax.optimization_barrier((everyone, sends[0], table, *second))
    tables = [table] + [swap(table, k) for k in (1, 2, 3)]
    near = swap(near, 1)
    mine = lax.all_to_all(everyone, "cols", split_axis=0, concat_axis=0, tiled=True)
    mine, *rest = lax.optimization_barrier((mine, *tables, *third))
    tables, third = rest[:4], rest[4:]
    masks = pl.pallas_call(
        functools.partial(mask_kernel, tiles, rows),
        out_shape=jax.ShapeDtypeStruct(((batches * owners * per + tiles * members) // CHUNK, kinds, CHUNK), f32),
        in_specs=[WHOLE] * 5,
        out_specs=WHOLE,
        compiler_params=PARAMS,
        cost_estimate=cost(1024),
        name="masks",
    )(arrived, *tables)
    pieces = pl.pallas_call(
        functools.partial(split_kernel, cuts),
        out_shape=jax.ShapeDtypeStruct((2 * members, cells), bf16),
        in_specs=[WHOLE] * (1 + len(cuts)),
        out_specs=WHOLE,
        compiler_params=PARAMS,
        name="split",
    )(state, near, *first, *second, *third)
    by_core, by_x = swap(mine, 1), swap(mine, 2)
    by_x, pieces, masks = lax.optimization_barrier((by_x, pieces, masks))
    by_both = swap(by_x, 1)
    return window_call(tiles, rows, mine, by_core, by_x, by_both, arrived, masks, pieces)


def innovations(prior_obs, observed, obs_noise, accepted):
    members = prior_obs.shape[0]
    mean_prior = jnp.mean(prior_obs, axis=0)
    spread = prior_obs - mean_prior
    spread_var = jnp.sum(spread * spread, axis=0) / (members - 1) + epsilon
    denominator = spread_var + obs_noise
    mean_shift = spread_var / denominator * (observed - mean_prior)
    factor = jnp.sqrt(obs_noise / denominator) - 1.0
    increment = accepted * (mean_shift + factor * spread)
    scaled = spread / ((members - 1) * spread_var)
    return (increment, scaled)


def plain(state, obs_value, obs_var, owner, tile_of, offsets, accept, loc_mask):
    col_devices = lax.axis_size("cols")
    mem_devices = lax.axis_size("mem")
    source = lax.axis_index("cols")
    mem_index = lax.axis_index("mem")
    batch_total, per_src = obs_value.shape
    pick_count = offsets.shape[2]
    members = state.shape[0] * mem_devices
    cell_count = state.shape[1] // mem_devices
    tiles_here = loc_mask.shape[0]
    tile_len = cell_count // tiles_here
    block_count = loc_mask.shape[2]
    batch_obs = per_src * col_devices
    block_len = batch_obs // block_count
    capacity = max(2, 2 * per_src // col_devices)
    slot_count = col_devices * capacity
    destination = owner[:, :, 0]
    ordinal = jnp.arange(per_src, dtype=jnp.int32)
    same_owner = destination[:, :, None] == destination[:, None, :]
    earlier = (ordinal[None, :] < ordinal[:, None])[None]
    slot_rank = jnp.sum((same_owner & earlier).astype(jnp.int32), axis=2)
    batch_rows = jnp.broadcast_to(
        jnp.arange(batch_total, dtype=jnp.int32)[:, None], destination.shape
    )
    position = jnp.broadcast_to(source * per_src + ordinal, destination.shape)
    fields = jnp.concatenate(
        [tile_of[:, :, None], accept[:, :, None], position[:, :, None], offsets], axis=2
    )
    blank_int = (
        jnp.zeros((batch_total, col_devices, capacity, 3 + pick_count), jnp.int32)
        .at[:, :, :, 2]
        .set(-1)
    )
    sent_int = blank_int.at[batch_rows, destination, slot_rank].set(fields)
    blank_val = (
        jnp.zeros((batch_total, col_devices, capacity, 2), jnp.float32).at[:, :, :, 1].set(1.0)
    )
    sent_val = blank_val.at[batch_rows, destination, slot_rank].set(
        jnp.stack([obs_value, obs_var], axis=2)
    )
    arrived_int = lax.all_to_all(sent_int, "cols", split_axis=1, concat_axis=1, tiled=True).reshape(
        batch_total, slot_count, 3 + pick_count
    )
    arrived_val = lax.all_to_all(sent_val, "cols", split_axis=1, concat_axis=1, tiled=True).reshape(
        batch_total, slot_count, 2
    )
    obs_tile = arrived_int[:, :, 0]
    obs_flag = arrived_int[:, :, 1].astype(jnp.float32)
    obs_pos = arrived_int[:, :, 2]
    obs_off = arrived_int[:, :, 3:]
    observed = arrived_val[:, :, 0]
    obs_noise = arrived_val[:, :, 1]
    targets = jnp.where(obs_pos >= 0, obs_pos, batch_obs)
    ensemble = lax.all_to_all(state, "mem", split_axis=1, concat_axis=0, tiled=True)
    for batch_no in range(batch_total):
        local_cell = (
            obs_tile[batch_no][:, None] * tile_len + obs_off[batch_no] - mem_index * cell_count
        )
        inside = (local_cell >= 0) & (local_cell < cell_count) & (obs_pos[batch_no] >= 0)[:, None]
        flat_cells = jnp.clip(local_cell, 0, cell_count - 1).reshape(-1)
        picked = jnp.take(ensemble, flat_cells, axis=1).reshape(members, slot_count, pick_count)
        prior_obs = lax.psum(
            jnp.sum(jnp.where(inside[None], picked, 0.0), axis=2) / pick_count, "mem"
        )
        increment, scaled = innovations(
            prior_obs, observed[batch_no], obs_noise[batch_no], obs_flag[batch_no]
        )
        blank_panel = jnp.zeros((members, batch_obs), jnp.float32)
        placed_inc = blank_panel.at[:, targets[batch_no]].add(increment, mode="drop")
        placed_scl = blank_panel.at[:, targets[batch_no]].add(scaled, mode="drop")
        inc_all, scl_all = lax.psum((placed_inc, placed_scl), "cols")
        mask_now = loc_mask[:, batch_no, :].astype(jnp.float32)
        mean_state = jnp.mean(ensemble, axis=0)
        deviation = (ensemble - mean_state).reshape(members, tiles_here, tile_len)
        per_block = jnp.einsum(
            "nbk,mbk->bnm",
            scl_all.reshape(members, block_count, block_len),
            inc_all.reshape(members, block_count, block_len),
            precision=EXACT,
        )
        mixing = jnp.einsum("tb,bnm->tnm", mask_now, per_block, precision=EXACT)
        change = jnp.einsum("tnm,nti->mti", mixing, deviation, precision=EXACT).reshape(
            members, cell_count
        )
        ensemble = ensemble + change
    return ensemble

def local(*arrays):
    state, obs_value, _, _, _, _, _, loc_mask = arrays
    per = obs_value.shape[1]
    owners, mem_devices = lax.axis_size("cols"), lax.axis_size("mem")
    tiles, batches, blocks = loc_mask.shape
    fits = (
        mem_devices == 4
        and owners == blocks == 8
        and per == LANES
        and batches == 4
        and tiles == 16
        and state.shape == (20, 64 * 512)
    )
    return fast(*arrays) if fits else plain(*arrays)


def solution(mesh):
    return jax.shard_map(
        local,
        mesh=mesh,
        in_specs=(
            P("mem", "cols"),
            P(None, "cols"),
            P(None, "cols"),
            P(None, "cols", None),
            P(None, "cols"),
            P(None, "cols", None),
            P(None, "cols"),
            P(("cols", "mem"), None, None),
        ),
        out_specs=P(None, ("cols", "mem")),
        check_vma=False,
    )
```

```python
import functools

import jax
import jax.numpy as jnp
from jax import lax
from jax.experimental import pallas as pl
from jax.experimental.pallas import tpu as pltpu
from jax.sharding import PartitionSpec as P

epsilon = 1e-05
EXACT = lax.Precision.HIGHEST
f32, bf16, i32 = jnp.float32, jnp.bfloat16, jnp.int32
LANES = 128
CHUNK = 256
TILE = 512
SWAPS = ((2, 0, 8), (3, 0, 8), (2, 8, 13), (3, 8, 13), (2, 13, 16), (3, 13, 16))
PAD = 24
WHOLE = pl.BlockSpec()
FAR = pl.BlockSpec(memory_space=pltpu.HBM)
PARAMS = pltpu.CompilerParams(vmem_limit_bytes=48 * 1024 * 1024)
ALONE = pltpu.CompilerParams(vmem_limit_bytes=64 * 1024 * 1024)
NEARLY = pltpu.CompilerParams(vmem_limit_bytes=64 * 1024 * 1024 - 200 * 1024)


def cost(amount):
    return pl.CostEstimate(flops=0, bytes_accessed=amount, transcendentals=0)


def iota(shape, axis):
    return lax.broadcasted_iota(i32, shape, axis)


def dot(a, b, dims):
    return lax.dot_general(a, b, ((dims[0], dims[1]), ((), ())), preferred_element_type=f32)


def two(x):
    high = x.astype(bf16)
    return high, (x - high.astype(f32)).astype(bf16)


def slot_rows(sid, slots):
    return jnp.where(iota((slots, sid.shape[1]), 0) == sid, 1.0, 0.0).astype(bf16)


def route_kernel(owners, slots_per, cuts, *refs):
    n = len(cuts)
    ins, state_ref, (msg_ref, sid_ref) = refs[0:7], refs[7], refs[8:10]
    sends, here, held, sems = refs[10 : 10 + n], refs[10 + n : 17 + n], refs[17 + n : 17 + 2 * n], refs[17 + 2 * n]
    cells = state_ref.shape[1] // 4
    mem = lax.axis_index("mem")
    copies = [pltpu.make_async_copy(a, b, sems.at[i]) for i, (a, b) in enumerate(zip(ins, here))]
    for copy in copies:
        copy.start()
    cutting = []
    for i, (k, begin, end) in enumerate(cuts):
        start = pl.multiple_of((mem ^ k) * cells + begin, LANES)
        cutting.append(pltpu.make_async_copy(state_ref.at[:, pl.ds(start, end - begin)], held[i], sems.at[7 + i]))
        cutting[-1].start()
    for copy in copies:
        copy.wait()
    owner_ref, tile_ref, off_ref, val_ref, var_ref, acc_ref, mask_ref = here
    batches, _, per = owner_ref.shape
    slots = owners * slots_per
    hot = [
        jnp.where(iota((owners, per), 0) == owner_ref[b], 1.0, 0.0) for b in range(batches)
    ]
    before = jnp.where(iota((per, per), 0) < iota((per, per), 1), 1.0, 0.0).astype(bf16)
    counts = dot(jnp.concatenate(hot, axis=0).astype(bf16), before, ((1,), (0,)))
    used = jnp.zeros((owners, 1), f32)
    total = jnp.zeros((16, slots), f32)
    for b in range(batches):
        own = owner_ref[b]
        rank = used + counts[b * owners : (b + 1) * owners]
        rank = jnp.sum(hot[b] * rank, axis=0, keepdims=True)
        used = used + jnp.sum(hot[b], axis=1, keepdims=True)
        sid = own * slots_per + rank.astype(i32)
        sid_ref[b : b + 1, :] = sid
        cells = tile_ref[b : b + 1, :] * 512 + off_ref[b]
        fields = jnp.concatenate(
            [(cells >> 7).astype(f32), (cells & 127).astype(f32), jnp.ones((8, per), f32)], axis=0
        ).astype(bf16)
        total = total + dot(fields, slot_rows(sid, slots), ((1,), (1,)))
    sending = [pltpu.make_async_copy(held[i], sends[i], sems.at[7 + n + i]) for i in range(n)]
    for copy_in, copy_out in zip(cutting, sending):
        copy_in.wait()
        copy_out.start()
    where = total[0:4] * 128.0 + total[4:8] + (total[8:12] - 1.0)
    tiles = mask_ref.shape[1]
    kinds = mask_ref.shape[0]
    spread_out = jnp.where(iota((kinds, LANES), 0) == (iota((kinds, LANES), 1) & (kinds - 1)), 1.0, 0.0)
    wide = dot(mask_ref[...].astype(bf16), spread_out.astype(bf16), ((0,), (0,)))
    group = LANES // kinds
    lane_tile = iota((tiles, LANES), 1) // kinds
    table = [
        jnp.sum(jnp.where(iota((tiles, LANES), 0) == lane_tile + r * group, wide, 0.0), axis=0, keepdims=True)
        for r in range(tiles // group)
    ]
    owner = jnp.concatenate([owner_ref[b] for b in range(batches)], axis=0)
    where_tile = (owner * 64 + tile_ref[...]).astype(f32)
    shared = jnp.concatenate(
        [val_ref[...], var_ref[...], acc_ref[...].astype(f32), where_tile] + table, axis=0
    )
    for c in range(owners):
        msg_ref[c, 0:4, :] = where[:, c * slots_per : (c + 1) * slots_per]
        msg_ref[c, 4:24, :] = shared
    for copy in sending:
        copy.wait()


def cut_kernel(cuts, state_ref, *refs):
    sends, sem = refs[:-1], refs[-1]
    cells = state_ref.shape[1] // 4
    mem = lax.axis_index("mem")
    copies = []
    for ref, (k, begin, end) in zip(sends, cuts):
        start = pl.multiple_of((mem ^ k) * cells + begin, LANES)
        copies.append(pltpu.make_async_copy(state_ref.at[:, pl.ds(start, end - begin)], ref, sem.at[len(copies)]))
        copies[-1].start()
    for copy in copies:
        copy.wait()


def prepare_kernel(state_ref, out_ref):
    rows = state_ref.shape[0]
    for i in range(state_ref.shape[1] // (2 * TILE)):
        left, right = (state_ref[:, j * TILE : (j + 1) * TILE] for j in (2 * i, 2 * i + 1))
        pair = jnp.concatenate([left, right], axis=0)
        high = pair.astype(bf16).astype(f32)
        out_ref[i * 4 * rows : (i + 1) * 4 * rows, :] = jnp.concatenate([high, pair - high], axis=0).astype(bf16)


def pick_kernel(rows, msg_ref, parts_ref, out_ref, table_ref, weight_ref):
    homes, _, slots_per = msg_ref.shape
    pairs = parts_ref.shape[0] // (4 * rows)
    below = jnp.where(iota((2 * rows, CHUNK), 0) >= rows, 1, 0)
    each = CHUNK // slots_per
    table_ref[...] = msg_ref[:, 20:24, :]
    for g in range(homes // each):
        cells = jnp.concatenate([msg_ref[g * each + i, 0:4, :] for i in range(each)], axis=1)
        cells = jnp.maximum(cells.astype(i32), 0)
        weight = jnp.zeros((TILE, CHUNK), f32)
        for p in range(4):
            weight = weight + jnp.where(iota((TILE, CHUNK), 0) == (cells[p : p + 1] & (TILE - 1)), 0.25, 0.0)
        weight_ref[...] = weight.astype(bf16)
        tile = (cells[0:1] >> 9) - below
        sums = dot(parts_ref[...], weight_ref[...], ((1,), (0,)))
        total = jnp.zeros((2 * rows, CHUNK), f32)
        for j in range(pairs):
            at = j * 4 * rows
            both = sums[at : at + 2 * rows] + sums[at + 2 * rows : at + 4 * rows]
            total = total + jnp.where(tile == 2 * j, both, 0.0)
        total = total[0:rows] + total[rows : 2 * rows]
        for i in range(each):
            out_ref[g * each + i] = total[:, i * slots_per : (i + 1) * slots_per]


def place_kernel(got_ref, sid_ref, out_ref):
    owners, rows, slots_per = got_ref.shape
    batches, per = sid_ref.shape
    slots = owners * slots_per
    fill = jnp.zeros((PAD - rows, slots), f32)
    got = jnp.concatenate([got_ref[c] for c in range(owners)], axis=1)
    got = jnp.concatenate([got, fill], axis=0)
    first = got.astype(bf16).astype(f32)
    rest = got - first
    second = rest.astype(bf16).astype(f32)
    parts = jnp.concatenate([first, second, rest - second], axis=0).astype(bf16)
    placed = []
    for b in range(batches):
        out = dot(parts, slot_rows(sid_ref[b : b + 1, :], slots), ((1,), (0,)))
        out = out[0:PAD] + out[PAD : 2 * PAD] + out[2 * PAD : 3 * PAD]
        placed.append(out[0:rows])
    placed = jnp.concatenate(placed, axis=0)
    for c in range(owners):
        out_ref[c] = placed


def fill_masks(tiles, members, kinds, info_ref, table, mask_ref):
    homes = info_ref.shape[0]
    mem = lax.axis_index("mem")
    device = lax.axis_index("cols") * lax.axis_size("mem") + mem
    obs_chunks = 4 * homes // 2
    for idx in range(homes // 2, mask_ref.shape[0]):
        if idx < obs_chunks:
            b, h = idx // 4, 2 * (idx % 4)
            where_tile = jnp.concatenate([info_ref[h, 16 + b : 17 + b, :], info_ref[h + 1, 16 + b : 17 + b, :]], axis=1)
            where_tile = where_tile.astype(i32)
        else:
            column = iota((1, CHUNK), 1) + (idx - obs_chunks) * CHUNK
            where_tile = jnp.zeros((1, CHUNK), i32) + device * tiles
            for t in range(1, tiles):
                where_tile = where_tile + jnp.where(column >= t * members, 1, 0)
        row = ((((where_tile >> 4) & 3) ^ mem) * homes + (where_tile >> 6)) * 4 + ((where_tile >> 2) & 3)
        hot = jnp.where(iota((LANES, CHUNK), 0) == row, 1.0, 0.0).astype(bf16)
        rows = dot(table, hot, ((0,), (0,)))
        out = jnp.zeros((kinds, CHUNK), f32)
        for g in range(LANES // kinds):
            out = out + jnp.where((where_tile & 3) == g, rows[g * kinds : (g + 1) * kinds], 0.0)
        mask_ref[idx] = out


def split_kernel(cuts, *refs):
    state, received, out_ref = refs[0], refs[1:-1], refs[-1]
    rows, total = received[0].shape
    here = pl.multiple_of(lax.axis_index("mem") * total, total)
    marks = sorted({cut[1] for cut in cuts} | {cut[2] for cut in cuts})
    for begin, end in zip(marks[:-1], marks[1:]):
        parts = [state[:, pl.ds(here + begin, end - begin)]]
        for k in (1, 2, 3):
            for ref, (to, first, last) in zip(received, cuts):
                if to == k and first <= begin and end <= last:
                    parts.append(ref[:, begin - first : end - first])
        high, low = two(jnp.concatenate(parts, axis=0))
        out_ref[0 : 4 * rows, begin:end] = high
        out_ref[4 * rows : 8 * rows, begin:end] = low


def mask_kernel(tiles, rows, info_ref, a_ref, b_ref, c_ref, d_ref, mask_ref):
    homes = info_ref.shape[0]
    table = [ref[h] for ref in (a_ref, b_ref, c_ref, d_ref) for h in range(homes)]
    table = jnp.concatenate(table, axis=0).astype(bf16)
    fill_masks(tiles, 4 * rows, mask_ref.shape[1], info_ref, table, mask_ref)


def window_kernel(tiles, rows, a_ref, b_ref, c_ref, d_ref, info_ref, mask_ref, ens_ref, out_ref, y_ref, w_ref, held_ref, sem):
    homes, all_rows, per = a_ref.shape
    batches = 4
    members = 4 * rows
    blocks = homes
    mem = lax.axis_index("mem")
    obs_chunks = batches * homes * per // CHUNK
    x_chunks = tiles * members // CHUNK
    for b in range(batches):
        for h in range(homes):
            chunk, place = b * (homes // 2) + h // 2, (h % 2) * per
            y_ref[chunk, :, place : place + per] = jnp.concatenate(
                [ref[h, b * rows : (b + 1) * rows, :] for ref in (a_ref, b_ref, c_ref, d_ref)], axis=0
            )
    member = iota((members, CHUNK), 0)
    for q in range(x_chunks):
        column = iota((1, CHUNK), 1) + q * CHUNK
        tile = jnp.zeros((1, CHUNK), i32)
        for t in range(1, tiles):
            tile = tile + jnp.where(column >= t * members, 1, 0)
        y_ref[obs_chunks + q] = jnp.where(member == column - tile * members, 1.0, 0.0)

    for b in range(batches):
        for g in range(homes // 2):
            def field(f):
                return jnp.concatenate(
                    [info_ref[h, 4 + 4 * f + b : 5 + 4 * f + b, :] for h in (2 * g, 2 * g + 1)], axis=1
                )

            prior = y_ref[b * (homes // 2) + g]
            mean = jnp.sum(prior, axis=0, keepdims=True) / members
            spread = prior - mean
            var = jnp.sum(spread * spread, axis=0, keepdims=True) / (members - 1) + epsilon
            noise = field(1)
            denominator = var + noise
            shift = var / denominator * (field(0) - mean)
            factor = jnp.sqrt(noise / denominator) - 1.0
            increment = field(2) * (shift + factor * spread)
            scaled = spread / ((members - 1) * var)
            ih, il = two(increment)
            sh, sl = two(scaled)
            for i in range(2):
                lanes = slice(i * per, (i + 1) * per)
                left = jnp.concatenate([ih[:, lanes], ih[:, lanes], il[:, lanes]], axis=1)
                right = jnp.concatenate([sh[:, lanes], sl[:, lanes], sh[:, lanes]], axis=1)
                block = dot(left, right, ((1,), (1,)))
                high = block.astype(bf16).astype(f32)
                block = jnp.concatenate([high, high, block - high], axis=1)
                h = 2 * g + i
                w_ref[h * members : (h + 1) * members, :] = block.astype(bf16)

        def update(idx, b=b):
            now = y_ref[idx]
            deviation = now - jnp.sum(now, axis=0, keepdims=True) / members
            dh, dl = two(deviation)
            moved = dot(w_ref[...], jnp.concatenate([dh, dl, dh], axis=0), ((1,), (0,)))
            for k in range(blocks):
                now = now + mask_ref[idx, b * blocks + k : b * blocks + k + 1, :] * moved[
                    k * members : (k + 1) * members
                ]
            y_ref[idx] = now

        for idx in range((b + 1) * (homes // 2), obs_chunks + x_chunks):
            update(idx)

    size = out_ref.shape[1] // tiles
    true, at = iota((members, members), 0), iota((members, members), 1)
    part = jnp.zeros((members, members), i32)
    for k in range(1, 4):
        part = part + jnp.where(at >= k * rows, 1, 0)
    order = jnp.where(true == at - part * rows + (part ^ mem) * rows, 1.0, 0.0)
    order = jnp.concatenate([order, order, order], axis=1).astype(bf16)
    flat = []
    for q in range(x_chunks):
        now = y_ref[obs_chunks + q]
        first = now.astype(bf16).astype(f32)
        rest = now - first
        second = rest.astype(bf16).astype(f32)
        stack = jnp.concatenate([first, second, rest - second], axis=0).astype(bf16)
        flat.append(dot(order, stack, ((1,), (0,))))
    flat = jnp.concatenate(flat, axis=1)
    copies = []
    for t in range(tiles):
        weight = flat[:, t * members : (t + 1) * members]
        high = weight.astype(bf16).astype(f32)
        weight = jnp.concatenate([high, high, weight - high], axis=1).astype(bf16)
        cells = slice(t * size, (t + 1) * size)
        ens_high, ens_low = ens_ref[0:members, cells], ens_ref[members : 2 * members, cells]
        held_ref[t] = dot(weight, jnp.concatenate([ens_high, ens_low, ens_high], axis=0), ((1,), (0,)))
        copies.append(pltpu.make_async_copy(held_ref.at[t], out_ref.at[:, cells], sem.at[t]))
        copies[-1].start()
    for copy in copies:
        copy.wait()


def window_call(tiles, rows, mine, by_core, by_x, by_both, about, masks, pieces):
    owners, _, per = mine.shape
    members, cells = pieces.shape[0] // 2, pieces.shape[1]
    chunks = masks.shape[0]
    return pl.pallas_call(
        functools.partial(window_kernel, tiles, rows),
        out_shape=jax.ShapeDtypeStruct((members, cells), f32),
        in_specs=[WHOLE] * 7,
        out_specs=FAR,
        scratch_shapes=[
            pltpu.VMEM((chunks, members, CHUNK), f32),
            pltpu.VMEM((owners * members, 3 * members), bf16),
            pltpu.VMEM((tiles, members, cells // tiles), f32),
            pltpu.SemaphoreType.DMA((tiles,)),
        ],
        compiler_params=PARAMS,
        name="window",
    )(mine, by_core, by_x, by_both, about, masks, pieces)


def fast(state, obs_value, obs_var, owner, tile_of, offsets, accept, loc_mask):
    owners = lax.axis_size("cols")
    mem_devices = lax.axis_size("mem")
    mem = lax.axis_index("mem")
    batches, per = obs_value.shape
    rows, slab = state.shape
    members = rows * mem_devices
    cells = slab // mem_devices
    tiles = loc_mask.shape[0]
    kinds = loc_mask.shape[1] * loc_mask.shape[2]
    cap = 2 * per // owners
    slots_per = batches * cap

    about = (
        owner.transpose(0, 2, 1),
        tile_of,
        offsets.transpose(0, 2, 1),
        obs_value,
        obs_var,
        accept,
        loc_mask.transpose(1, 2, 0).reshape(kinds, tiles),
    )
    cuts = [(1, 0, cells)] + [(k, cells * a // 16, cells * b // 16) for k, a, b in SWAPS]
    sooner, later = cuts[1:3], cuts[0:1] + cuts[3:]
    msg, sid, *first = pl.pallas_call(
        functools.partial(route_kernel, owners, slots_per, sooner),
        out_shape=(
            jax.ShapeDtypeStruct((owners, 24, slots_per), f32),
            jax.ShapeDtypeStruct((batches, per), i32),
            *(jax.ShapeDtypeStruct((rows, end - begin), f32) for _, begin, end in sooner),
        ),
        in_specs=[FAR] * 8,
        out_specs=(WHOLE,) * 2 + (FAR,) * len(sooner),
        scratch_shapes=[pltpu.VMEM(a.shape, a.dtype) for a in about]
        + [pltpu.VMEM((rows, end - begin), f32) for _, begin, end in sooner]
        + [pltpu.SemaphoreType.DMA((7 + 2 * len(sooner),))],
        compiler_params=ALONE,
        name="route",
    )(*about, state)
    state, msg = lax.optimization_barrier((state, msg))
    arrived = lax.all_to_all(msg, "cols", split_axis=0, concat_axis=0, tiled=True)

    sends = pl.pallas_call(
        functools.partial(cut_kernel, later),
        out_shape=tuple(jax.ShapeDtypeStruct((rows, end - begin), f32) for _, begin, end in later),
        in_specs=[WHOLE],
        out_specs=(FAR,) * len(later),
        scratch_shapes=[pltpu.SemaphoreType.DMA((len(later),))],
        compiler_params=NEARLY,
        cost_estimate=cost(1024),
        name="cut",
    )(state)
    parts = pl.pallas_call(
        prepare_kernel,
        out_shape=jax.ShapeDtypeStruct((slab // TILE * 2 * rows, TILE), bf16),
        in_specs=[WHOLE],
        out_specs=WHOLE,
        compiler_params=PARAMS,
        cost_estimate=cost(1024),
        name="prepare",
    )(state)

    def swap(array, k):
        return lax.ppermute(array, "mem", [(i, i ^ k) for i in range(4)])

    first = [swap(array, k) for array, (k, _, _) in zip(first, sooner)]
    far = [swap(array, k) for array, (k, _, _) in zip(sends[1:], later[1:])]
    second, third = far[0:2], far[2:]
    priors, table = pl.pallas_call(
        functools.partial(pick_kernel, rows),
        out_shape=(
            jax.ShapeDtypeStruct((owners, rows, slots_per), f32),
            jax.ShapeDtypeStruct((owners, 4, LANES), f32),
        ),
        in_specs=[WHOLE] * 2,
        out_specs=(WHOLE,) * 2,
        scratch_shapes=[pltpu.VMEM((TILE, CHUNK), bf16)],
        compiler_params=PARAMS,
        cost_estimate=cost(1024),
        name="pick",
    )(arrived, parts)
    at_home = lax.all_to_all(priors, "cols", split_axis=0, concat_axis=0, tiled=True)
    at_home, *first = lax.optimization_barrier((at_home, *first))
    everyone = pl.pallas_call(
        place_kernel,
        out_shape=jax.ShapeDtypeStruct((owners, batches * rows, per), f32),
        in_specs=[WHOLE] * 2,
        out_specs=WHOLE,
        compiler_params=PARAMS,
        name="place",
    )(at_home, sid)
    everyone, near, table, *second = lax.optimization_barrier((everyone, sends[0], table, *second))
    tables = [table] + [swap(table, k) for k in (1, 2, 3)]
    near = swap(near, 1)
    mine = lax.all_to_all(everyone, "cols", split_axis=0, concat_axis=0, tiled=True)
    mine, *rest = lax.optimization_barrier((mine, *tables, *third))
    tables, third = rest[:4], rest[4:]
    masks = pl.pallas_call(
        functools.partial(mask_kernel, tiles, rows),
        out_shape=jax.ShapeDtypeStruct(((batches * owners * per + tiles * members) // CHUNK, kinds, CHUNK), f32),
        in_specs=[WHOLE] * 5,
        out_specs=WHOLE,
        compiler_params=PARAMS,
        cost_estimate=cost(1024),
        name="masks",
    )(arrived, *tables)
    pieces = pl.pallas_call(
        functools.partial(split_kernel, cuts),
        out_shape=jax.ShapeDtypeStruct((2 * members, cells), bf16),
        in_specs=[WHOLE] * (1 + len(cuts)),
        out_specs=WHOLE,
        compiler_params=PARAMS,
        name="split",
    )(state, near, *first, *second, *third)
    by_core, by_x = swap(mine, 1), swap(mine, 2)
    by_x, pieces, masks = lax.optimization_barrier((by_x, pieces, masks))
    by_both = swap(by_x, 1)
    return window_call(tiles, rows, mine, by_core, by_x, by_both, arrived, masks, pieces)


def innovations(prior_obs, observed, obs_noise, accepted):
    members = prior_obs.shape[0]
    mean_prior = jnp.mean(prior_obs, axis=0)
    spread = prior_obs - mean_prior
    spread_var = jnp.sum(spread * spread, axis=0) / (members - 1) + epsilon
    denominator = spread_var + obs_noise
    mean_shift = spread_var / denominator * (observed - mean_prior)
    factor = jnp.sqrt(obs_noise / denominator) - 1.0
    increment = accepted * (mean_shift + factor * spread)
    scaled = spread / ((members - 1) * spread_var)
    return (increment, scaled)


def plain(state, obs_value, obs_var, owner, tile_of, offsets, accept, loc_mask):
    col_devices = lax.axis_size("cols")
    mem_devices = lax.axis_size("mem")
    source = lax.axis_index("cols")
    mem_index = lax.axis_index("mem")
    batch_total, per_src = obs_value.shape
    pick_count = offsets.shape[2]
    members = state.shape[0] * mem_devices
    cell_count = state.shape[1] // mem_devices
    tiles_here = loc_mask.shape[0]
    tile_len = cell_count // tiles_here
    block_count = loc_mask.shape[2]
    batch_obs = per_src * col_devices
    block_len = batch_obs // block_count
    capacity = max(2, 2 * per_src // col_devices)
    slot_count = col_devices * capacity
    destination = owner[:, :, 0]
    ordinal = jnp.arange(per_src, dtype=jnp.int32)
    same_owner = destination[:, :, None] == destination[:, None, :]
    earlier = (ordinal[None, :] < ordinal[:, None])[None]
    slot_rank = jnp.sum((same_owner & earlier).astype(jnp.int32), axis=2)
    batch_rows = jnp.broadcast_to(
        jnp.arange(batch_total, dtype=jnp.int32)[:, None], destination.shape
    )
    position = jnp.broadcast_to(source * per_src + ordinal, destination.shape)
    fields = jnp.concatenate(
        [tile_of[:, :, None], accept[:, :, None], position[:, :, None], offsets], axis=2
    )
    blank_int = (
        jnp.zeros((batch_total, col_devices, capacity, 3 + pick_count), jnp.int32)
        .at[:, :, :, 2]
        .set(-1)
    )
    sent_int = blank_int.at[batch_rows, destination, slot_rank].set(fields)
    blank_val = (
        jnp.zeros((batch_total, col_devices, capacity, 2), jnp.float32).at[:, :, :, 1].set(1.0)
    )
    sent_val = blank_val.at[batch_rows, destination, slot_rank].set(
        jnp.stack([obs_value, obs_var], axis=2)
    )
    arrived_int = lax.all_to_all(sent_int, "cols", split_axis=1, concat_axis=1, tiled=True).reshape(
        batch_total, slot_count, 3 + pick_count
    )
    arrived_val = lax.all_to_all(sent_val, "cols", split_axis=1, concat_axis=1, tiled=True).reshape(
        batch_total, slot_count, 2
    )
    obs_tile = arrived_int[:, :, 0]
    obs_flag = arrived_int[:, :, 1].astype(jnp.float32)
    obs_pos = arrived_int[:, :, 2]
    obs_off = arrived_int[:, :, 3:]
    observed = arrived_val[:, :, 0]
    obs_noise = arrived_val[:, :, 1]
    targets = jnp.where(obs_pos >= 0, obs_pos, batch_obs)
    ensemble = lax.all_to_all(state, "mem", split_axis=1, concat_axis=0, tiled=True)
    for batch_no in range(batch_total):
        local_cell = (
            obs_tile[batch_no][:, None] * tile_len + obs_off[batch_no] - mem_index * cell_count
        )
        inside = (local_cell >= 0) & (local_cell < cell_count) & (obs_pos[batch_no] >= 0)[:, None]
        flat_cells = jnp.clip(local_cell, 0, cell_count - 1).reshape(-1)
        picked = jnp.take(ensemble, flat_cells, axis=1).reshape(members, slot_count, pick_count)
        prior_obs = lax.psum(
            jnp.sum(jnp.where(inside[None], picked, 0.0), axis=2) / pick_count, "mem"
        )
        increment, scaled = innovations(
            prior_obs, observed[batch_no], obs_noise[batch_no], obs_flag[batch_no]
        )
        blank_panel = jnp.zeros((members, batch_obs), jnp.float32)
        placed_inc = blank_panel.at[:, targets[batch_no]].add(increment, mode="drop")
        placed_scl = blank_panel.at[:, targets[batch_no]].add(scaled, mode="drop")
        inc_all, scl_all = lax.psum((placed_inc, placed_scl), "cols")
        mask_now = loc_mask[:, batch_no, :].astype(jnp.float32)
        mean_state = jnp.mean(ensemble, axis=0)
        deviation = (ensemble - mean_state).reshape(members, tiles_here, tile_len)
        per_block = jnp.einsum(
            "nbk,mbk->bnm",
            scl_all.reshape(members, block_count, block_len),
            inc_all.reshape(members, block_count, block_len),
            precision=EXACT,
        )
        mixing = jnp.einsum("tb,bnm->tnm", mask_now, per_block, precision=EXACT)
        change = jnp.einsum("tnm,nti->mti", mixing, deviation, precision=EXACT).reshape(
            members, cell_count
        )
        ensemble = ensemble + change
    return ensemble

def local(*arrays):
    state, obs_value, _, _, _, _, _, loc_mask = arrays
    per = obs_value.shape[1]
    owners, mem_devices = lax.axis_size("cols"), lax.axis_size("mem")
    tiles, batches, blocks = loc_mask.shape
    fits = (
        mem_devices == 4
        and owners == blocks == 8
        and per == LANES
        and batches == 4
        and tiles == 16
        and state.shape == (20, 64 * 512)
    )
    return fast(*arrays) if fits else plain(*arrays)


def solution(mesh):
    return jax.shard_map(
        local,
        mesh=mesh,
        in_specs=(
            P("mem", "cols"),
            P(None, "cols"),
            P(None, "cols"),
            P(None, "cols", None),
            P(None, "cols"),
            P(None, "cols", None),
            P(None, "cols"),
            P(("cols", "mem"), None, None),
        ),
        out_specs=P(None, ("cols", "mem")),
        check_vma=False,
    )
```

```python
import functools

import jax
import jax.numpy as jnp
from jax import lax
from jax.experimental import pallas as pl
from jax.experimental.pallas import tpu as pltpu
from jax.sharding import PartitionSpec as P

epsilon = 1e-05
EXACT = lax.Precision.HIGHEST
f32, bf16, i32 = jnp.float32, jnp.bfloat16, jnp.int32
LANES = 128
CHUNK = 256
TILE = 512
SWAPS = ((2, 0, 8), (3, 0, 8), (2, 8, 13), (3, 8, 13), (2, 13, 16), (3, 13, 16))
PAD = 24
WHOLE = pl.BlockSpec()
FAR = pl.BlockSpec(memory_space=pltpu.HBM)
PARAMS = pltpu.CompilerParams(vmem_limit_bytes=48 * 1024 * 1024)
ALONE = pltpu.CompilerParams(vmem_limit_bytes=64 * 1024 * 1024)
NEARLY = pltpu.CompilerParams(vmem_limit_bytes=64 * 1024 * 1024 - 200 * 1024)


def cost(amount):
    return pl.CostEstimate(flops=0, bytes_accessed=amount, transcendentals=0)


def iota(shape, axis):
    return lax.broadcasted_iota(i32, shape, axis)


def dot(a, b, dims):
    return lax.dot_general(a, b, ((dims[0], dims[1]), ((), ())), preferred_element_type=f32)


def two(x):
    high = x.astype(bf16)
    return high, (x - high.astype(f32)).astype(bf16)


def slot_rows(sid, slots):
    return jnp.where(iota((slots, sid.shape[1]), 0) == sid, 1.0, 0.0).astype(bf16)


def route_kernel(owners, slots_per, cuts, *refs):
    n = len(cuts)
    ins, state_ref, (msg_ref, sid_ref) = refs[0:7], refs[7], refs[8:10]
    sends, here, held, sems = refs[10 : 10 + n], refs[10 + n : 17 + n], refs[17 + n : 17 + 2 * n], refs[17 + 2 * n]
    cells = state_ref.shape[1] // 4
    mem = lax.axis_index("mem")
    copies = [pltpu.make_async_copy(a, b, sems.at[i]) for i, (a, b) in enumerate(zip(ins, here))]
    for copy in copies:
        copy.start()
    cutting = []
    for i, (k, begin, end) in enumerate(cuts):
        start = pl.multiple_of((mem ^ k) * cells + begin, LANES)
        cutting.append(pltpu.make_async_copy(state_ref.at[:, pl.ds(start, end - begin)], held[i], sems.at[7 + i]))
        cutting[-1].start()
    for copy in copies:
        copy.wait()
    owner_ref, tile_ref, off_ref, val_ref, var_ref, acc_ref, mask_ref = here
    batches, _, per = owner_ref.shape
    slots = owners * slots_per
    hot = [
        jnp.where(iota((owners, per), 0) == owner_ref[b], 1.0, 0.0) for b in range(batches)
    ]
    before = jnp.where(iota((per, per), 0) < iota((per, per), 1), 1.0, 0.0).astype(bf16)
    counts = dot(jnp.concatenate(hot, axis=0).astype(bf16), before, ((1,), (0,)))
    used = jnp.zeros((owners, 1), f32)
    total = jnp.zeros((16, slots), f32)
    for b in range(batches):
        own = owner_ref[b]
        rank = used + counts[b * owners : (b + 1) * owners]
        rank = jnp.sum(hot[b] * rank, axis=0, keepdims=True)
        used = used + jnp.sum(hot[b], axis=1, keepdims=True)
        sid = own * slots_per + rank.astype(i32)
        sid_ref[b : b + 1, :] = sid
        cells = tile_ref[b : b + 1, :] * 512 + off_ref[b]
        fields = jnp.concatenate(
            [(cells >> 7).astype(f32), (cells & 127).astype(f32), jnp.ones((8, per), f32)], axis=0
        ).astype(bf16)
        total = total + dot(fields, slot_rows(sid, slots), ((1,), (1,)))
    sending = [pltpu.make_async_copy(held[i], sends[i], sems.at[7 + n + i]) for i in range(n)]
    for copy_in, copy_out in zip(cutting, sending):
        copy_in.wait()
        copy_out.start()
    where = total[0:4] * 128.0 + total[4:8] + (total[8:12] - 1.0)
    tiles = mask_ref.shape[1]
    kinds = mask_ref.shape[0]
    spread_out = jnp.where(iota((kinds, LANES), 0) == (iota((kinds, LANES), 1) & (kinds - 1)), 1.0, 0.0)
    wide = dot(mask_ref[...].astype(bf16), spread_out.astype(bf16), ((0,), (0,)))
    group = LANES // kinds
    lane_tile = iota((tiles, LANES), 1) // kinds
    table = [
        jnp.sum(jnp.where(iota((tiles, LANES), 0) == lane_tile + r * group, wide, 0.0), axis=0, keepdims=True)
        for r in range(tiles // group)
    ]
    owner = jnp.concatenate([owner_ref[b] for b in range(batches)], axis=0)
    where_tile = (owner * 64 + tile_ref[...]).astype(f32)
    shared = jnp.concatenate(
        [val_ref[...], var_ref[...], acc_ref[...].astype(f32), where_tile] + table, axis=0
    )
    for c in range(owners):
        msg_ref[c, 0:4, :] = where[:, c * slots_per : (c + 1) * slots_per]
        msg_ref[c, 4:24, :] = shared
    for copy in sending:
        copy.wait()


def cut_kernel(cuts, state_ref, *refs):
    n = len(cuts)
    sends, held, sems = refs[0:n], refs[n : 2 * n], refs[2 * n]
    cells = state_ref.shape[1] // 4
    mem = lax.axis_index("mem")
    taken, sent = [], []
    for i, (k, begin, end) in enumerate(cuts):
        start = pl.multiple_of((mem ^ k) * cells + begin, LANES)
        taken.append(pltpu.make_async_copy(state_ref.at[:, pl.ds(start, end - begin)], held[i], sems.at[i]))
        sent.append(pltpu.make_async_copy(held[i], sends[i], sems.at[n + i]))
        taken[i].start()
    for copy_in, copy_out in zip(taken, sent):
        copy_in.wait()
        copy_out.start()
    for copy in sent:
        copy.wait()


def prepare_kernel(state_ref, out_ref):
    rows = state_ref.shape[0]
    for i in range(state_ref.shape[1] // (2 * TILE)):
        left, right = (state_ref[:, j * TILE : (j + 1) * TILE] for j in (2 * i, 2 * i + 1))
        pair = jnp.concatenate([left, right], axis=0)
        high = pair.astype(bf16).astype(f32)
        out_ref[i * 4 * rows : (i + 1) * 4 * rows, :] = jnp.concatenate([high, pair - high], axis=0).astype(bf16)


def pick_kernel(rows, msg_ref, parts_ref, out_ref, table_ref, weight_ref):
    homes, _, slots_per = msg_ref.shape
    pairs = parts_ref.shape[0] // (4 * rows)
    below = jnp.where(iota((2 * rows, CHUNK), 0) >= rows, 1, 0)
    each = CHUNK // slots_per
    table_ref[...] = msg_ref[:, 20:24, :]
    for g in range(homes // each):
        cells = jnp.concatenate([msg_ref[g * each + i, 0:4, :] for i in range(each)], axis=1)
        cells = jnp.maximum(cells.astype(i32), 0)
        weight = jnp.zeros((TILE, CHUNK), f32)
        for p in range(4):
            weight = weight + jnp.where(iota((TILE, CHUNK), 0) == (cells[p : p + 1] & (TILE - 1)), 0.25, 0.0)
        weight_ref[...] = weight.astype(bf16)
        tile = (cells[0:1] >> 9) - below
        sums = dot(parts_ref[...], weight_ref[...], ((1,), (0,)))
        total = jnp.zeros((2 * rows, CHUNK), f32)
        for j in range(pairs):
            at = j * 4 * rows
            both = sums[at : at + 2 * rows] + sums[at + 2 * rows : at + 4 * rows]
            total = total + jnp.where(tile == 2 * j, both, 0.0)
        total = total[0:rows] + total[rows : 2 * rows]
        for i in range(each):
            out_ref[g * each + i] = total[:, i * slots_per : (i + 1) * slots_per]


def place_kernel(got_ref, sid_ref, out_ref):
    owners, rows, slots_per = got_ref.shape
    batches, per = sid_ref.shape
    slots = owners * slots_per
    fill = jnp.zeros((PAD - rows, slots), f32)
    got = jnp.concatenate([got_ref[c] for c in range(owners)], axis=1)
    got = jnp.concatenate([got, fill], axis=0)
    first = got.astype(bf16).astype(f32)
    rest = got - first
    second = rest.astype(bf16).astype(f32)
    parts = jnp.concatenate([first, second, rest - second], axis=0).astype(bf16)
    placed = []
    for b in range(batches):
        out = dot(parts, slot_rows(sid_ref[b : b + 1, :], slots), ((1,), (0,)))
        out = out[0:PAD] + out[PAD : 2 * PAD] + out[2 * PAD : 3 * PAD]
        placed.append(out[0:rows])
    placed = jnp.concatenate(placed, axis=0)
    for c in range(owners):
        out_ref[c] = placed


def fill_masks(tiles, members, kinds, info_ref, table, mask_ref):
    homes = info_ref.shape[0]
    mem = lax.axis_index("mem")
    device = lax.axis_index("cols") * lax.axis_size("mem") + mem
    obs_chunks = 4 * homes // 2
    for idx in range(homes // 2, mask_ref.shape[0]):
        if idx < obs_chunks:
            b, h = idx // 4, 2 * (idx % 4)
            where_tile = jnp.concatenate([info_ref[h, 16 + b : 17 + b, :], info_ref[h + 1, 16 + b : 17 + b, :]], axis=1)
            where_tile = where_tile.astype(i32)
        else:
            column = iota((1, CHUNK), 1) + (idx - obs_chunks) * CHUNK
            where_tile = jnp.zeros((1, CHUNK), i32) + device * tiles
            for t in range(1, tiles):
                where_tile = where_tile + jnp.where(column >= t * members, 1, 0)
        row = ((((where_tile >> 4) & 3) ^ mem) * homes + (where_tile >> 6)) * 4 + ((where_tile >> 2) & 3)
        hot = jnp.where(iota((LANES, CHUNK), 0) == row, 1.0, 0.0).astype(bf16)
        rows = dot(table, hot, ((0,), (0,)))
        out = jnp.zeros((kinds, CHUNK), f32)
        for g in range(LANES // kinds):
            out = out + jnp.where((where_tile & 3) == g, rows[g * kinds : (g + 1) * kinds], 0.0)
        mask_ref[idx] = out


def split_kernel(cuts, *refs):
    state, received, out_ref = refs[0], refs[1:-1], refs[-1]
    rows, total = received[0].shape
    here = pl.multiple_of(lax.axis_index("mem") * total, total)
    marks = sorted({cut[1] for cut in cuts} | {cut[2] for cut in cuts})
    for begin, end in zip(marks[:-1], marks[1:]):
        parts = [state[:, pl.ds(here + begin, end - begin)]]
        for k in (1, 2, 3):
            for ref, (to, first, last) in zip(received, cuts):
                if to == k and first <= begin and end <= last:
                    parts.append(ref[:, begin - first : end - first])
        high, low = two(jnp.concatenate(parts, axis=0))
        out_ref[0 : 4 * rows, begin:end] = high
        out_ref[4 * rows : 8 * rows, begin:end] = low


def mask_kernel(tiles, rows, info_ref, a_ref, b_ref, c_ref, d_ref, mask_ref):
    homes = info_ref.shape[0]
    table = [ref[h] for ref in (a_ref, b_ref, c_ref, d_ref) for h in range(homes)]
    table = jnp.concatenate(table, axis=0).astype(bf16)
    fill_masks(tiles, 4 * rows, mask_ref.shape[1], info_ref, table, mask_ref)


def window_kernel(tiles, rows, a_ref, b_ref, c_ref, d_ref, info_ref, mask_ref, ens_ref, out_ref, y_ref, w_ref, held_ref, sem):
    homes, all_rows, per = a_ref.shape
    batches = 4
    members = 4 * rows
    blocks = homes
    mem = lax.axis_index("mem")
    obs_chunks = batches * homes * per // CHUNK
    x_chunks = tiles * members // CHUNK
    for b in range(batches):
        for h in range(homes):
            chunk, place = b * (homes // 2) + h // 2, (h % 2) * per
            y_ref[chunk, :, place : place + per] = jnp.concatenate(
                [ref[h, b * rows : (b + 1) * rows, :] for ref in (a_ref, b_ref, c_ref, d_ref)], axis=0
            )
    member = iota((members, CHUNK), 0)
    for q in range(x_chunks):
        column = iota((1, CHUNK), 1) + q * CHUNK
        tile = jnp.zeros((1, CHUNK), i32)
        for t in range(1, tiles):
            tile = tile + jnp.where(column >= t * members, 1, 0)
        y_ref[obs_chunks + q] = jnp.where(member == column - tile * members, 1.0, 0.0)

    for b in range(batches):
        for g in range(homes // 2):
            def field(f):
                return jnp.concatenate(
                    [info_ref[h, 4 + 4 * f + b : 5 + 4 * f + b, :] for h in (2 * g, 2 * g + 1)], axis=1
                )

            prior = y_ref[b * (homes // 2) + g]
            mean = jnp.sum(prior, axis=0, keepdims=True) / members
            spread = prior - mean
            var = jnp.sum(spread * spread, axis=0, keepdims=True) / (members - 1) + epsilon
            noise = field(1)
            denominator = var + noise
            shift = var / denominator * (field(0) - mean)
            factor = jnp.sqrt(noise / denominator) - 1.0
            increment = field(2) * (shift + factor * spread)
            scaled = spread / ((members - 1) * var)
            ih, il = two(increment)
            sh, sl = two(scaled)
            for i in range(2):
                lanes = slice(i * per, (i + 1) * per)
                left = jnp.concatenate([ih[:, lanes], ih[:, lanes], il[:, lanes]], axis=1)
                right = jnp.concatenate([sh[:, lanes], sl[:, lanes], sh[:, lanes]], axis=1)
                block = dot(left, right, ((1,), (1,)))
                high = block.astype(bf16).astype(f32)
                block = jnp.concatenate([high, high, block - high], axis=1)
                h = 2 * g + i
                w_ref[h * members : (h + 1) * members, :] = block.astype(bf16)

        def update(idx, b=b):
            now = y_ref[idx]
            deviation = now - jnp.sum(now, axis=0, keepdims=True) / members
            dh, dl = two(deviation)
            moved = dot(w_ref[...], jnp.concatenate([dh, dl, dh], axis=0), ((1,), (0,)))
            for k in range(blocks):
                now = now + mask_ref[idx, b * blocks + k : b * blocks + k + 1, :] * moved[
                    k * members : (k + 1) * members
                ]
            y_ref[idx] = now

        for idx in range((b + 1) * (homes // 2), obs_chunks + x_chunks):
            update(idx)

    size = out_ref.shape[1] // tiles
    true, at = iota((members, members), 0), iota((members, members), 1)
    part = jnp.zeros((members, members), i32)
    for k in range(1, 4):
        part = part + jnp.where(at >= k * rows, 1, 0)
    order = jnp.where(true == at - part * rows + (part ^ mem) * rows, 1.0, 0.0)
    order = jnp.concatenate([order, order, order], axis=1).astype(bf16)
    flat = []
    for q in range(x_chunks):
        now = y_ref[obs_chunks + q]
        first = now.astype(bf16).astype(f32)
        rest = now - first
        second = rest.astype(bf16).astype(f32)
        stack = jnp.concatenate([first, second, rest - second], axis=0).astype(bf16)
        flat.append(dot(order, stack, ((1,), (0,))))
    flat = jnp.concatenate(flat, axis=1)
    copies = []
    for t in range(tiles):
        weight = flat[:, t * members : (t + 1) * members]
        high = weight.astype(bf16).astype(f32)
        weight = jnp.concatenate([high, high, weight - high], axis=1).astype(bf16)
        cells = slice(t * size, (t + 1) * size)
        ens_high, ens_low = ens_ref[0:members, cells], ens_ref[members : 2 * members, cells]
        held_ref[t] = dot(weight, jnp.concatenate([ens_high, ens_low, ens_high], axis=0), ((1,), (0,)))
        copies.append(pltpu.make_async_copy(held_ref.at[t], out_ref.at[:, cells], sem.at[t]))
        copies[-1].start()
    for copy in copies:
        copy.wait()


def window_call(tiles, rows, mine, by_core, by_x, by_both, about, masks, pieces):
    owners, _, per = mine.shape
    members, cells = pieces.shape[0] // 2, pieces.shape[1]
    chunks = masks.shape[0]
    return pl.pallas_call(
        functools.partial(window_kernel, tiles, rows),
        out_shape=jax.ShapeDtypeStruct((members, cells), f32),
        in_specs=[WHOLE] * 7,
        out_specs=FAR,
        scratch_shapes=[
            pltpu.VMEM((chunks, members, CHUNK), f32),
            pltpu.VMEM((owners * members, 3 * members), bf16),
            pltpu.VMEM((tiles, members, cells // tiles), f32),
            pltpu.SemaphoreType.DMA((tiles,)),
        ],
        compiler_params=PARAMS,
        name="window",
    )(mine, by_core, by_x, by_both, about, masks, pieces)


def fast(state, obs_value, obs_var, owner, tile_of, offsets, accept, loc_mask):
    owners = lax.axis_size("cols")
    mem_devices = lax.axis_size("mem")
    mem = lax.axis_index("mem")
    batches, per = obs_value.shape
    rows, slab = state.shape
    members = rows * mem_devices
    cells = slab // mem_devices
    tiles = loc_mask.shape[0]
    kinds = loc_mask.shape[1] * loc_mask.shape[2]
    cap = 2 * per // owners
    slots_per = batches * cap

    about = (
        owner.transpose(0, 2, 1),
        tile_of,
        offsets.transpose(0, 2, 1),
        obs_value,
        obs_var,
        accept,
        loc_mask.transpose(1, 2, 0).reshape(kinds, tiles),
    )
    cuts = [(1, 0, cells)] + [(k, cells * a // 16, cells * b // 16) for k, a, b in SWAPS]
    sooner, later = cuts[1:3], cuts[0:1] + cuts[3:]
    msg, sid, *first = pl.pallas_call(
        functools.partial(route_kernel, owners, slots_per, sooner),
        out_shape=(
            jax.ShapeDtypeStruct((owners, 24, slots_per), f32),
            jax.ShapeDtypeStruct((batches, per), i32),
            *(jax.ShapeDtypeStruct((rows, end - begin), f32) for _, begin, end in sooner),
        ),
        in_specs=[FAR] * 8,
        out_specs=(WHOLE,) * 2 + (FAR,) * len(sooner),
        scratch_shapes=[pltpu.VMEM(a.shape, a.dtype) for a in about]
        + [pltpu.VMEM((rows, end - begin), f32) for _, begin, end in sooner]
        + [pltpu.SemaphoreType.DMA((7 + 2 * len(sooner),))],
        compiler_params=ALONE,
        name="route",
    )(*about, state)
    state, msg = lax.optimization_barrier((state, msg))
    arrived = lax.all_to_all(msg, "cols", split_axis=0, concat_axis=0, tiled=True)

    sends = pl.pallas_call(
        functools.partial(cut_kernel, later),
        out_shape=tuple(jax.ShapeDtypeStruct((rows, end - begin), f32) for _, begin, end in later),
        in_specs=[FAR],
        out_specs=(FAR,) * len(later),
        scratch_shapes=[pltpu.VMEM((rows, end - begin), f32) for _, begin, end in later]
        + [pltpu.SemaphoreType.DMA((2 * len(later),))],
        compiler_params=NEARLY,
        cost_estimate=cost(1024),
        name="cut",
    )(state)
    parts = pl.pallas_call(
        prepare_kernel,
        out_shape=jax.ShapeDtypeStruct((slab // TILE * 2 * rows, TILE), bf16),
        in_specs=[WHOLE],
        out_specs=WHOLE,
        compiler_params=PARAMS,
        cost_estimate=cost(1024),
        name="prepare",
    )(state)

    def swap(array, k):
        return lax.ppermute(array, "mem", [(i, i ^ k) for i in range(4)])

    first = [swap(array, k) for array, (k, _, _) in zip(first, sooner)]
    far = [swap(array, k) for array, (k, _, _) in zip(sends[1:], later[1:])]
    second, third = far[0:2], far[2:]
    priors, table = pl.pallas_call(
        functools.partial(pick_kernel, rows),
        out_shape=(
            jax.ShapeDtypeStruct((owners, rows, slots_per), f32),
            jax.ShapeDtypeStruct((owners, 4, LANES), f32),
        ),
        in_specs=[WHOLE] * 2,
        out_specs=(WHOLE,) * 2,
        scratch_shapes=[pltpu.VMEM((TILE, CHUNK), bf16)],
        compiler_params=PARAMS,
        cost_estimate=cost(1024),
        name="pick",
    )(arrived, parts)
    at_home = lax.all_to_all(priors, "cols", split_axis=0, concat_axis=0, tiled=True)
    at_home, *first = lax.optimization_barrier((at_home, *first))
    everyone = pl.pallas_call(
        place_kernel,
        out_shape=jax.ShapeDtypeStruct((owners, batches * rows, per), f32),
        in_specs=[WHOLE] * 2,
        out_specs=WHOLE,
        compiler_params=PARAMS,
        name="place",
    )(at_home, sid)
    everyone, near, table, *second = lax.optimization_barrier((everyone, sends[0], table, *second))
    tables = [table] + [swap(table, k) for k in (1, 2, 3)]
    near = swap(near, 1)
    mine = lax.all_to_all(everyone, "cols", split_axis=0, concat_axis=0, tiled=True)
    mine, *rest = lax.optimization_barrier((mine, *tables, *third))
    tables, third = rest[:4], rest[4:]
    masks = pl.pallas_call(
        functools.partial(mask_kernel, tiles, rows),
        out_shape=jax.ShapeDtypeStruct(((batches * owners * per + tiles * members) // CHUNK, kinds, CHUNK), f32),
        in_specs=[WHOLE] * 5,
        out_specs=WHOLE,
        compiler_params=PARAMS,
        cost_estimate=cost(1024),
        name="masks",
    )(arrived, *tables)
    pieces = pl.pallas_call(
        functools.partial(split_kernel, cuts),
        out_shape=jax.ShapeDtypeStruct((2 * members, cells), bf16),
        in_specs=[WHOLE] * (1 + len(cuts)),
        out_specs=WHOLE,
        compiler_params=PARAMS,
        name="split",
    )(state, near, *first, *second, *third)
    by_core, by_x = swap(mine, 1), swap(mine, 2)
    by_x, pieces, masks = lax.optimization_barrier((by_x, pieces, masks))
    by_both = swap(by_x, 1)
    return window_call(tiles, rows, mine, by_core, by_x, by_both, arrived, masks, pieces)


def innovations(prior_obs, observed, obs_noise, accepted):
    members = prior_obs.shape[0]
    mean_prior = jnp.mean(prior_obs, axis=0)
    spread = prior_obs - mean_prior
    spread_var = jnp.sum(spread * spread, axis=0) / (members - 1) + epsilon
    denominator = spread_var + obs_noise
    mean_shift = spread_var / denominator * (observed - mean_prior)
    factor = jnp.sqrt(obs_noise / denominator) - 1.0
    increment = accepted * (mean_shift + factor * spread)
    scaled = spread / ((members - 1) * spread_var)
    return (increment, scaled)


def plain(state, obs_value, obs_var, owner, tile_of, offsets, accept, loc_mask):
    col_devices = lax.axis_size("cols")
    mem_devices = lax.axis_size("mem")
    source = lax.axis_index("cols")
    mem_index = lax.axis_index("mem")
    batch_total, per_src = obs_value.shape
    pick_count = offsets.shape[2]
    members = state.shape[0] * mem_devices
    cell_count = state.shape[1] // mem_devices
    tiles_here = loc_mask.shape[0]
    tile_len = cell_count // tiles_here
    block_count = loc_mask.shape[2]
    batch_obs = per_src * col_devices
    block_len = batch_obs // block_count
    capacity = max(2, 2 * per_src // col_devices)
    slot_count = col_devices * capacity
    destination = owner[:, :, 0]
    ordinal = jnp.arange(per_src, dtype=jnp.int32)
    same_owner = destination[:, :, None] == destination[:, None, :]
    earlier = (ordinal[None, :] < ordinal[:, None])[None]
    slot_rank = jnp.sum((same_owner & earlier).astype(jnp.int32), axis=2)
    batch_rows = jnp.broadcast_to(
        jnp.arange(batch_total, dtype=jnp.int32)[:, None], destination.shape
    )
    position = jnp.broadcast_to(source * per_src + ordinal, destination.shape)
    fields = jnp.concatenate(
        [tile_of[:, :, None], accept[:, :, None], position[:, :, None], offsets], axis=2
    )
    blank_int = (
        jnp.zeros((batch_total, col_devices, capacity, 3 + pick_count), jnp.int32)
        .at[:, :, :, 2]
        .set(-1)
    )
    sent_int = blank_int.at[batch_rows, destination, slot_rank].set(fields)
    blank_val = (
        jnp.zeros((batch_total, col_devices, capacity, 2), jnp.float32).at[:, :, :, 1].set(1.0)
    )
    sent_val = blank_val.at[batch_rows, destination, slot_rank].set(
        jnp.stack([obs_value, obs_var], axis=2)
    )
    arrived_int = lax.all_to_all(sent_int, "cols", split_axis=1, concat_axis=1, tiled=True).reshape(
        batch_total, slot_count, 3 + pick_count
    )
    arrived_val = lax.all_to_all(sent_val, "cols", split_axis=1, concat_axis=1, tiled=True).reshape(
        batch_total, slot_count, 2
    )
    obs_tile = arrived_int[:, :, 0]
    obs_flag = arrived_int[:, :, 1].astype(jnp.float32)
    obs_pos = arrived_int[:, :, 2]
    obs_off = arrived_int[:, :, 3:]
    observed = arrived_val[:, :, 0]
    obs_noise = arrived_val[:, :, 1]
    targets = jnp.where(obs_pos >= 0, obs_pos, batch_obs)
    ensemble = lax.all_to_all(state, "mem", split_axis=1, concat_axis=0, tiled=True)
    for batch_no in range(batch_total):
        local_cell = (
            obs_tile[batch_no][:, None] * tile_len + obs_off[batch_no] - mem_index * cell_count
        )
        inside = (local_cell >= 0) & (local_cell < cell_count) & (obs_pos[batch_no] >= 0)[:, None]
        flat_cells = jnp.clip(local_cell, 0, cell_count - 1).reshape(-1)
        picked = jnp.take(ensemble, flat_cells, axis=1).reshape(members, slot_count, pick_count)
        prior_obs = lax.psum(
            jnp.sum(jnp.where(inside[None], picked, 0.0), axis=2) / pick_count, "mem"
        )
        increment, scaled = innovations(
            prior_obs, observed[batch_no], obs_noise[batch_no], obs_flag[batch_no]
        )
        blank_panel = jnp.zeros((members, batch_obs), jnp.float32)
        placed_inc = blank_panel.at[:, targets[batch_no]].add(increment, mode="drop")
        placed_scl = blank_panel.at[:, targets[batch_no]].add(scaled, mode="drop")
        inc_all, scl_all = lax.psum((placed_inc, placed_scl), "cols")
        mask_now = loc_mask[:, batch_no, :].astype(jnp.float32)
        mean_state = jnp.mean(ensemble, axis=0)
        deviation = (ensemble - mean_state).reshape(members, tiles_here, tile_len)
        per_block = jnp.einsum(
            "nbk,mbk->bnm",
            scl_all.reshape(members, block_count, block_len),
            inc_all.reshape(members, block_count, block_len),
            precision=EXACT,
        )
        mixing = jnp.einsum("tb,bnm->tnm", mask_now, per_block, precision=EXACT)
        change = jnp.einsum("tnm,nti->mti", mixing, deviation, precision=EXACT).reshape(
            members, cell_count
        )
        ensemble = ensemble + change
    return ensemble

def local(*arrays):
    state, obs_value, _, _, _, _, _, loc_mask = arrays
    per = obs_value.shape[1]
    owners, mem_devices = lax.axis_size("cols"), lax.axis_size("mem")
    tiles, batches, blocks = loc_mask.shape
    fits = (
        mem_devices == 4
        and owners == blocks == 8
        and per == LANES
        and batches == 4
        and tiles == 16
        and state.shape == (20, 64 * 512)
    )
    return fast(*arrays) if fits else plain(*arrays)


def solution(mesh):
    return jax.shard_map(
        local,
        mesh=mesh,
        in_specs=(
            P("mem", "cols"),
            P(None, "cols"),
            P(None, "cols"),
            P(None, "cols", None),
            P(None, "cols"),
            P(None, "cols", None),
            P(None, "cols"),
            P(("cols", "mem"), None, None),
        ),
        out_specs=P(None, ("cols", "mem")),
        check_vma=False,
    )
```
